32 devices in a mesh: row: 8 (over y, x, core), col: 4 (over z).
Axes of the slice: x: 2, y: 2, z: 4, core: 2. Of those that a mesh axis runs over, the one named last changes fastest.
Arguments:
- features: bfloat16 [16384, 256], P(('col', 'row')), may hold values from -6 to 6
- degree: int32 [16384], P(('col', 'row')), may hold values from 1 to 8
- cotangent: bfloat16 [16384, 256], P(('col', 'row')), may hold values from -6 to 6
- tile_values: bfloat16 [12288, 128, 128], P(('col', 'row')), may hold values from -0.078125 to 0.078125
- tile_row: int32 [12288], P(('col', 'row')), may hold values from 0 to 32, as said below
- tile_col: int32 [12288], P(('col', 'row')), may hold values from 0 to 15, as said below
- w_self: bfloat16 [256, 256], replicated, may hold values from -0.375 to 0.375
- w_neigh: bfloat16 [256, 256], replicated, may hold values from -0.375 to 0.375
- bias: float32 [256], replicated, may hold values from -3 to 3
Outputs:
- hidden: bfloat16 [16384, 256], P(('col', 'row'))
- grad_x: bfloat16 [16384, 256], P(('col', 'row'))
- grad_self: float32 [256, 256], replicated
- grad_neigh: float32 [256, 256], replicated
- grad_bias: float32 [256], replicated
The draws below stay inside these ranges and needn't reach their ends.
Inputs may be any that keep to these rules, and one draw needn't show every extreme that they name: `tile_row`: on each device the live slots come first and the rest hold 32; no two live slots of one device share a tile row and tile column; every device has between 96 and 384 live slots, and some device has all 384 live. `tile_col`: empty slots hold 0.
All inputs are finite; a program needn't handle non-finite values.
Results may differ from the reference program's by a relative error of at most 0.0054.
Values may be sent and summed in bfloat16 or wider, within the bound.
No kernel may reach another device: no remote copies, remote signals or barrier semaphores. Data moves between devices by JAX's collectives and lax.ppermute only.
A program may use at most 256 MiB of HBM per device.

```python
import jax
import jax.numpy as jnp
from jax import lax

D = 256
TILE = 128
NODE_DEV = 512
TILES = 384
NODES = 16384
N_ROW = 8
N_COL = 4


def tile_layout(key):
    dest_tiles = N_ROW * NODE_DEV // TILE
    src_tiles = N_COL * NODE_DEV // TILE
    devices = N_ROW * N_COL
    cells = dest_tiles * src_tiles
    keys = jax.random.split(key, devices + 2)
    picks = jax.vmap(lambda sub: jax.random.permutation(sub, cells)[:TILES])(keys[:devices])
    live_count = jax.random.randint(keys[devices], (devices,), TILES // 4, TILES + 1)
    full_one = jax.random.randint(keys[devices + 1], (), 0, devices)
    live_count = jnp.where(jnp.arange(devices) == full_one, TILES, live_count)
    used = jnp.arange(TILES)[None, :] < live_count[:, None]
    rows = jnp.where(used, picks // src_tiles, dest_tiles)
    cols = jnp.where(used, picks % src_tiles, 0)
    return (rows.reshape(-1).astype(jnp.int32), cols.reshape(-1).astype(jnp.int32))


def draw_tile_row(key, part):
    return tile_layout(key)[0]


def draw_tile_col(key, part):
    return tile_layout(key)[1]


def place_ends(values, rng, smallest, largest):
    longest = values.shape.index(max(values.shape))
    spots = []
    for shift in (0, 1):
        where = [jax.random.randint(jax.random.fold_in(rng, axis), (), 0, length) for axis, length in enumerate(values.shape)]
        where[longest] = (where[longest] + shift) % values.shape[longest]
        spots.append(tuple(where))
    return values.at[spots[0]].set(smallest).at[spots[1]].set(largest)


def steps_of(key, extent, cuts, smallest, high):
    gain = 1.0
    for axis_at, shards_of in cuts:
        draws = jax.random.uniform(jax.random.fold_in(jax.random.fold_in(key, 6), axis_at), (shards_of,), jnp.float32, smallest / len(cuts), high / len(cuts))
        gain = gain * jnp.repeat(jnp.exp(draws), extent[axis_at] // shards_of).reshape((-1,) + (1,) * (len(extent) - 1 - axis_at))
    return gain


def gaussian(key, shape, width, bound, cuts=(), kind=jnp.bfloat16):
    drawn = jax.random.normal(key, shape, jnp.float32) * width
    if len(cuts) > 0:
        drawn = steps_of(key, shape, cuts, -0.22, 0.18) * drawn
    return jnp.clip(drawn, min=-bound, max=bound).astype(kind)


def setup_inputs(seed: int = 0) -> dict:
    key_list = jax.random.split(jax.random.key(seed), 10)
    return {
        "features": gaussian(key_list[0], (NODES, D), 1.0, 6.0, ((0, 32),)),
        "degree": place_ends(jax.random.randint(key_list[1], (NODES,), 1, 9), jax.random.fold_in(key_list[1], 1), 1, 8).astype(jnp.int32),
        "cotangent": gaussian(key_list[2], (NODES, D), 1.0, 6.0, ((0, 32),)),
        "tile_values": gaussian(key_list[3], (N_ROW * N_COL * TILES, TILE, TILE), (N_ROW * 1024 * TILES // NODE_DEV) ** -0.5, 0.078125, ((0, 32),)),
        "tile_row": draw_tile_row(jax.random.fold_in(key_list[9], 71), 0),
        "tile_col": draw_tile_col(jax.random.fold_in(key_list[9], 71), 0),
        "w_self": gaussian(key_list[6], (D, D), D ** -0.5, 0.375),
        "w_neigh": gaussian(key_list[7], (D, D), D ** -0.5, 0.375),
        "bias": gaussian(key_list[8], (D,), 0.5, 3.0, (), jnp.float32),
    }


def reference(features, degree, cotangent, tile_values, tile_row, tile_col, w_self, w_neigh, bias):
    dest_tiles = N_ROW * NODE_DEV // TILE
    src_tiles = N_COL * NODE_DEV // TILE
    grid = features.reshape(N_COL, N_ROW, NODE_DEV, D)
    values = tile_values.reshape(N_COL * N_ROW, TILES, TILE, TILE)
    rows = tile_row.reshape(N_COL * N_ROW, TILES)
    cols = tile_col.reshape(N_COL * N_ROW, TILES)

    def forward_step(carry, index):
        c_idx = index // N_ROW
        r_idx = index % N_ROW
        source = lax.dynamic_index_in_dim(grid, r_idx, 1, keepdims=False)
        source = source.reshape(src_tiles, TILE, D)
        picked = source[cols[index]]
        prods = jnp.einsum("tuv,tvd->tud", values[index].astype(jnp.float32), picked.astype(jnp.float32))
        part = jax.ops.segment_sum(prods, rows[index], num_segments=dest_tiles)
        carry = carry.at[c_idx].add(part.reshape(N_ROW * NODE_DEV, D))
        return carry, None

    start = jnp.zeros((N_COL, N_ROW * NODE_DEV, D), jnp.float32)
    agg, _ = lax.scan(forward_step, start, jnp.arange(N_COL * N_ROW, dtype=jnp.int32))
    agg = agg.reshape(NODES, D)
    scale = degree.astype(jnp.float32)[:, None]
    neigh_mean = (agg / scale).astype(jnp.bfloat16)
    pre = jnp.dot(features, w_self, preferred_element_type=jnp.float32)
    pre = pre + jnp.dot(neigh_mean, w_neigh, preferred_element_type=jnp.float32) + bias[None, :]
    sig = jax.nn.sigmoid(pre)
    hidden = (pre * sig).astype(jnp.bfloat16)
    d_pre = (cotangent.astype(jnp.float32) * sig * (1.0 + pre * (1.0 - sig))).astype(jnp.bfloat16)
    grad_self = jnp.dot(features.T, d_pre, preferred_element_type=jnp.float32)
    grad_neigh = jnp.dot(neigh_mean.T, d_pre, preferred_element_type=jnp.float32)
    grad_bias = jnp.sum(d_pre.astype(jnp.float32), axis=0)
    d_agg = (jnp.dot(d_pre, w_neigh.T, preferred_element_type=jnp.float32) / scale).astype(jnp.bfloat16)
    dgrid = d_agg.reshape(N_COL, N_ROW * NODE_DEV, D)

    def backward_step(carry, index):
        c_idx = index // N_ROW
        r_idx = index % N_ROW
        dest = lax.dynamic_index_in_dim(dgrid, c_idx, 0, keepdims=False).reshape(dest_tiles, TILE, D)
        live = (rows[index] < dest_tiles).astype(jnp.float32)
        picked = dest[jnp.minimum(rows[index], dest_tiles - 1)]
        back = jnp.einsum("tuv,tud->tvd", values[index].astype(jnp.float32), picked.astype(jnp.float32))
        back = back * live[:, None, None]
        part = jax.ops.segment_sum(back, cols[index], num_segments=src_tiles).reshape(N_COL, NODE_DEV, D)
        current = lax.dynamic_index_in_dim(carry, r_idx, 1, keepdims=False)
        carry = lax.dynamic_update_index_in_dim(carry, current + part, r_idx, 1)
        return carry, None

    start_back = jnp.zeros((N_COL, N_ROW, NODE_DEV, D), jnp.float32)
    back_all, _ = lax.scan(backward_step, start_back, jnp.arange(N_COL * N_ROW, dtype=jnp.int32))
    grad_x = jnp.dot(d_pre, w_self.T, preferred_element_type=jnp.float32) + back_all.reshape(NODES, D)
    return hidden, grad_x.astype(jnp.bfloat16), grad_self, grad_neigh, grad_bias
```

```python
import jax
import jax.numpy as jnp
from jax import lax
from jax.experimental import pallas as pl
from jax.experimental.pallas import tpu as pltpu
from jax.sharding import PartitionSpec as P

F32 = jnp.float32
BF16 = jnp.bfloat16
MIB = 1 << 20
RESIDENT_BYTES = 20 * MIB
PARTS = 2
BIAS_ROWS = 16


def vmem():
    return pl.BlockSpec(memory_space=pltpu.VMEM)


def params(limit_mib):
    return pltpu.CompilerParams(vmem_limit_bytes=limit_mib * MIB)


def sds(shape, dtype):
    return jax.ShapeDtypeStruct(shape, dtype)


def densify(tile_values, tile_row, tile_col, place, n_row, n_col, per_dev, resident):
    slots, tile, _ = tile_values.shape
    chips = n_row // 2
    rows = n_row * per_dev
    cols = n_col * per_dev
    cells = rows * cols

    def kernel(row_ref, col_ref, place_ref, values_ref, dense_ref, table, blank, sem):
        blank[...] = jnp.zeros_like(blank)
        chip = place_ref[0] // 2
        core = place_ref[0] % 2
        col_at = place_ref[1]

        def clear(i, carry):
            for k in range(8):
                table[i * 8 + k] = slots
            return carry

        lax.fori_loop(0, cells // 8, clear, 0)

        def note(i, carry):
            for k in range(4):
                at = i * 4 + k
                table[row_ref[at] * cols + col_ref[at]] = at
            return carry

        lax.fori_loop(0, slots // 4, note, 0)

        def fill(i, carry):
            slot = table[i]
            t = i // cols
            s = i % cols
            owner = t // per_dev
            block = ((owner % 2) ^ core) * chips + ((owner // 2) ^ chip)
            u = (block * per_dev + t % per_dev) * tile
            v = (((s // per_dev) ^ col_at) * per_dev + s % per_dev) * tile
            where = dense_ref.at[
                pl.ds(pl.multiple_of(u, tile), tile), pl.ds(pl.multiple_of(v, tile), tile)
            ]

            @pl.when(slot < slots)
            def _():
                pltpu.make_async_copy(values_ref.at[slot], where, sem).start()

            @pl.when(slot >= slots)
            def _():
                pltpu.make_async_copy(blank, where, sem).start()

            return carry

        lax.fori_loop(0, cells, fill, 0)
        pltpu.make_async_copy(dense_ref, dense_ref, sem).wait()

    shape = (rows * tile, cols * tile)
    out_shape = pltpu.VMEM(shape, BF16) if resident else sds(shape, BF16)
    return pl.pallas_call(
        kernel,
        out_shape=out_shape,
        grid_spec=pltpu.PrefetchScalarGridSpec(
            num_scalar_prefetch=3,
            grid=(),
            in_specs=[pl.BlockSpec(memory_space=pl.ANY)],
            out_specs=vmem() if resident else pl.BlockSpec(memory_space=pl.ANY),
            scratch_shapes=[
                pltpu.SMEM((cells + cols,), jnp.int32),
                pltpu.VMEM((tile, tile), BF16),
                pltpu.SemaphoreType.DMA,
            ],
        ),
        compiler_params=params(8),
        name="densify",
    )(tile_row, tile_col, place, tile_values)


def pinned(dense, resident):
    return pltpu.with_memory_space_constraint(dense, pltpu.VMEM) if resident else dense


def forward(dense, pieces, first, count, dtype, resident):
    n_col = len(pieces)
    nodes, wide = pieces[0].shape
    cols = n_col * nodes

    def kernel(*refs):
        dense_ref, piece_refs, out_ref, source = refs[0], refs[1 : 1 + n_col], refs[-2], refs[-1]
        step = pl.program_id(0)

        @pl.when(step == 0)
        def _():
            for m in range(n_col):
                source[m * nodes : (m + 1) * nodes, :] = piece_refs[m][...]

        if resident:
            at = pl.multiple_of((first + step) * nodes, nodes)
            block = dense_ref[pl.ds(at, nodes), :]
        else:
            block = dense_ref[...]
        out_ref[0] = jnp.dot(block, source[...], preferred_element_type=F32).astype(dtype)

    spec = vmem() if resident else pl.BlockSpec((nodes, cols), lambda i: (i + first, 0))
    return pl.pallas_call(
        kernel,
        out_shape=sds((count, nodes, wide), dtype),
        grid=(count,),
        in_specs=[spec] + [pl.BlockSpec((nodes, wide), lambda i: (0, 0))] * n_col,
        out_specs=pl.BlockSpec((1, nodes, wide), lambda i: (i, 0, 0)),
        scratch_shapes=[pltpu.VMEM((cols, wide), BF16)],
        compiler_params=params(32),
        name="forward",
    )(pinned(dense, resident), *pieces)


def add_parts(keep, got):
    chips, nodes, wide = keep.shape

    def kernel(keep_ref, got_ref, *out_refs):
        for j in range(1, chips):
            out_refs[j - 1][...] = (keep_ref[j] + got_ref[j].astype(F32)).astype(BF16)

    return pl.pallas_call(
        kernel,
        out_shape=[sds((nodes, wide), BF16)] * (chips - 1),
        in_specs=[vmem()] * 2,
        out_specs=[vmem()] * (chips - 1),
        compiler_params=params(16),
        name="add_parts",
    )(keep, got)


def middle(features, scale, cotangent, w_self, w_neigh, bias, parts, n_row):
    nodes, width = features.shape
    chips = n_row // 2
    count = len(parts)
    wide = width // count
    share = width // n_row
    flat = []
    for keep, got, arrivals in parts:
        flat += [keep, got, *arrivals]
    each = len(flat) // count
    extra = 2 * share + BIAS_ROWS

    def kernel(*refs):
        feat_ref, scale_ref, cot_ref, ws_ref, wn_ref, bias_ref = refs[:6]
        part_refs = refs[6 : 6 + len(flat)]
        hidden_ref, d_pre_ref = refs[6 + len(flat) : 8 + len(flat)]
        send_refs = refs[8 + len(flat) : 8 + len(flat) + chips]
        rest_refs = refs[8 + len(flat) + chips :]
        inv = scale_ref[...]
        sums = []
        for h in range(count):
            mine = part_refs[h * each : (h + 1) * each]
            total = mine[0][0] + mine[1][0].astype(F32)
            for ref in mine[2:]:
                total = total + ref[...].astype(F32)
            sums.append(total)
        agg = jnp.concatenate(sums, axis=1) if count > 1 else sums[0]
        neigh_mean = (agg / inv).astype(BF16)
        features_now = feat_ref[...]
        pre = jnp.dot(features_now, ws_ref[...], preferred_element_type=F32)
        pre = pre + jnp.dot(neigh_mean, wn_ref[...], preferred_element_type=F32) + bias_ref[...]
        sig = jax.nn.sigmoid(pre)
        hidden_ref[...] = (pre * sig).astype(BF16)
        d_pre = (cot_ref[...].astype(F32) * sig * (1.0 + pre * (1.0 - sig))).astype(BF16)
        d_pre_ref[...] = d_pre
        d_agg = lax.dot_general(
            d_pre, wn_ref[...], (((1,), (1,)), ((), ())), preferred_element_type=F32
        )
        d_agg = jnp.transpose(d_agg / inv).astype(BF16)
        over = (((0,), (0,)), ((), ()))
        grad_self = lax.dot_general(features_now, d_pre, over, preferred_element_type=F32)
        grad_neigh = lax.dot_general(neigh_mean, d_pre, over, preferred_element_type=F32)
        grads = jnp.concatenate([grad_self, grad_neigh], axis=1).astype(BF16)
        bias_sum = jnp.sum(d_pre.astype(F32), axis=0, keepdims=True)
        bias_row = jnp.concatenate([bias_sum, bias_sum], axis=1).astype(BF16)
        bias_rows = jnp.broadcast_to(bias_row, (BIAS_ROWS, 2 * width))
        place_chip = lax.axis_index("row") // 2
        place_core = lax.axis_index("row") % 2
        grads_ref = rest_refs[-1]
        grads_ref[...] = grads.astype(F32)
        for j in range(chips):
            send_refs[j][0:wide, :] = d_agg[0:wide]
            for k in range(2):
                owner = (place_chip ^ j) * 2 + (place_core ^ k)
                at = pl.multiple_of(owner * share, share)
                low = wide + k * share
                send_refs[j][low : low + share, :] = grads_ref[pl.ds(at, share), :].astype(BF16)
            send_refs[j][wide + 2 * share :, :] = bias_rows
        for h in range(1, count):
            rest_refs[h - 1][...] = d_agg[h * wide : (h + 1) * wide]

    first_two = [pl.BlockSpec((1, nodes, wide), lambda i: (0, 0, 0))] * 2
    whole = lambda shape: pl.BlockSpec(shape, lambda i: (0,) * len(shape))
    part_specs = (first_two + [whole((nodes, wide))] * (each - 2)) * count
    outs = (
        [sds((nodes, width), BF16)] * 2
        + [sds((wide + extra, nodes), BF16)] * chips
        + [sds((wide, nodes), BF16)] * (count - 1)
    )
    args = [features, scale, cotangent, w_self, w_neigh, bias]
    res = pl.pallas_call(
        kernel,
        out_shape=outs,
        grid=(1,),
        in_specs=[whole(a.shape) for a in args] + part_specs,
        out_specs=[whole(o.shape) for o in outs],
        scratch_shapes=[pltpu.VMEM((width, 2 * width), F32)],
        compiler_params=params(32),
        name="middle",
    )(*args, *flat)
    return res[0], res[1], res[2 : 2 + chips], res[2 + chips :]


def backward(dense, pieces, n_col, wide, share, resident):
    n_row = len(pieces)
    nodes = pieces[0].shape[1]
    rows = n_row * nodes
    height = pieces[0].shape[0]
    extra = share + BIAS_ROWS if share else 0

    def kernel(*refs):
        dense_ref, piece_refs = refs[0], refs[1 : 1 + n_row]
        out_refs = refs[1 + n_row : 1 + n_row + n_col]
        total_ref = refs[1 + n_row + n_col] if share else None
        stacked = refs[-1]
        step = pl.program_id(0)

        @pl.when(step == 0)
        def _():
            for b in range(n_row):
                stacked[:, b * nodes : (b + 1) * nodes] = piece_refs[b][0:wide, :]
            if share:
                chips = n_row // 2
                total = jnp.zeros((share, nodes), F32)
                bias_total = jnp.zeros((BIAS_ROWS, nodes), F32)
                for b in range(n_row):
                    low = wide + (b // chips) * share
                    total = total + piece_refs[b][low : low + share, :].astype(F32)
                    bias_total = bias_total + piece_refs[b][wide + 2 * share :, :].astype(F32)
                total_ref[0:share, :] = total
                total_ref[share:, :] = bias_total
                for m in range(1, n_col):
                    out_refs[m][wide : wide + share, :] = total.astype(BF16)
                    out_refs[m][wide + share :, :] = bias_total.astype(BF16)

        for m in range(n_col):

            @pl.when(step == m)
            def _():
                if resident:
                    block = dense_ref[:, m * nodes : (m + 1) * nodes]
                else:
                    block = dense_ref[...]
                out = jnp.dot(stacked[...], block, preferred_element_type=F32)
                out_refs[m][0:wide, :] = out.astype(out_refs[m].dtype)

    spec = vmem() if resident else pl.BlockSpec((rows, nodes), lambda i: (0, i))
    whole = lambda shape: pl.BlockSpec(shape, lambda i: (0,) * len(shape))
    outs = [sds((wide, nodes), F32)] + [sds((wide + extra, nodes), BF16)] * (n_col - 1)
    if share:
        outs.append(sds((extra, nodes), F32))
    res = pl.pallas_call(
        kernel,
        out_shape=outs,
        grid=(n_col,),
        in_specs=[spec] + [whole((height, nodes))] * n_row,
        out_specs=[whole(o.shape) for o in outs],
        scratch_shapes=[pltpu.VMEM((wide, rows), BF16)],
        compiler_params=params(36),
        name="backward",
    )(pinned(dense, resident), *pieces)
    return res[0], res[1:n_col], (res[n_col] if share else None)


def share_total(total, arrivals, wide):
    height, nodes = total.shape

    def kernel(total_ref, *refs):
        out_ref = refs[-1]
        acc = total_ref[...]
        for ref in refs[:-1]:
            acc = acc + ref[wide : wide + height, :].astype(F32)
        out_ref[...] = acc

    return pl.pallas_call(
        kernel,
        out_shape=sds((height, nodes), F32),
        in_specs=[vmem()] * (1 + len(arrivals)),
        out_specs=vmem(),
        compiler_params=params(8),
        name="share_total",
    )(total, *arrivals)


def weight_grads(shares, n_row):
    share = shares[0].shape[0]
    width = shares[0].shape[1] // 2
    chips = n_row // 2

    def kernel(*refs):
        self_ref, neigh_ref = refs[-2:]
        chip = lax.axis_index("row") // 2
        core = lax.axis_index("row") % 2
        for b in range(n_row):
            owner = (chip ^ (b % chips)) * 2 + (core ^ (b // chips))
            at = pl.multiple_of(owner * share, share)
            self_ref[pl.ds(at, share), :] = refs[b][:, 0:width]
            neigh_ref[pl.ds(at, share), :] = refs[b][:, width:]

    return pl.pallas_call(
        kernel,
        out_shape=[sds((width, width), F32)] * 2,
        in_specs=[vmem()] * n_row,
        out_specs=[vmem()] * 2,
        compiler_params=params(8),
        name="weight_grads",
    )(*shares)


def finish(d_pre, w_self, owns, arrivals):
    nodes, width = d_pre.shape
    count = len(owns)
    wide = width // count
    others = len(arrivals[0])
    flat = list(owns) + [a for part in arrivals for a in part]

    def kernel(d_pre_ref, ws_ref, *refs):
        out_ref = refs[-1]
        direct = lax.dot_general(
            d_pre_ref[...], ws_ref[...], (((1,), (1,)), ((), ())), preferred_element_type=F32
        )
        for h in range(count):
            acc = refs[h][...]
            for ref in refs[count + h * others : count + (h + 1) * others]:
                acc = acc + ref[0:wide, :].astype(F32)
            low = h * wide
            out = direct[:, low : low + wide] + jnp.transpose(acc)
            out_ref[:, low : low + wide] = out.astype(BF16)

    return pl.pallas_call(
        kernel,
        out_shape=sds((nodes, width), BF16),
        in_specs=[vmem()] * (2 + len(flat)),
        out_specs=vmem(),
        compiler_params=params(16),
        name="finish",
    )(d_pre, w_self, *flat)


def swap(x, axis, mask):
    size = lax.axis_size(axis)
    return lax.ppermute(x, axis, [(i, i ^ mask) for i in range(size)])


def far_first(n):
    return sorted(range(1, n), key=lambda m: -bin(m).count("1") * n - m)


def body(features, degree, cotangent, tile_values, tile_row, tile_col, w_self, w_neigh, bias):
    nodes, width = features.shape
    tile = tile_values.shape[1]
    n_row = lax.axis_size("row")
    n_col = lax.axis_size("col")
    chips = n_row // 2
    per_dev = nodes // tile
    wide = width // PARTS
    share = width // n_row
    resident = n_row * nodes * n_col * nodes * 2 <= RESIDENT_BYTES

    sources = []
    for h in range(PARTS):
        own = features[:, h * wide : (h + 1) * wide]
        pieces = {0: own}
        for m in far_first(n_col):
            pieces[m] = swap(own, "col", m)
        sources.append([pieces[m] for m in range(n_col)])

    place = jnp.stack([lax.axis_index("row"), lax.axis_index("col")]).astype(jnp.int32)
    dense = densify(tile_values, tile_row, tile_col, place, n_row, n_col, per_dev, resident)
    scale = degree.astype(F32)[:, None]

    parts = []
    for h in range(PARTS):
        give = forward(dense, sources[h], chips, chips, BF16, resident)
        got = swap(give, "row", 1)
        keep = forward(dense, sources[h], 0, chips, F32, resident)
        sends = add_parts(keep, got)
        arrivals = [swap(sends[j - 1], "row", 2 * j) for j in range(1, chips)]
        parts.append((keep, got, arrivals))

    hidden, d_pre, first_sends, later = middle(
        features, scale, cotangent, w_self, w_neigh, bias[None, :], parts, n_row
    )

    owns, backs = [], []
    for h in range(PARTS):
        if h == 0:
            mine = [first_sends[0]] + [
                swap(first_sends[j], "row", 2 * j) for j in range(1, chips)
            ]
        else:
            mine = [later[h - 1]] + [swap(later[h - 1], "row", 2 * j) for j in range(1, chips)]
        siblings = [swap(piece, "row", 1) for piece in mine]
        own, sends, total = backward(
            dense, mine + siblings, n_col, wide, share if h == 0 else 0, resident
        )
        arrived = {m: swap(sends[m - 1], "col", m) for m in far_first(n_col)}
        arrived = [arrived[m] for m in range(1, n_col)]
        owns.append(own)
        backs.append(arrived)
        if h == 0:
            summed = share_total(total, arrived, wide)
            grad_bias = summed[share, 0:width]
            piece = summed[0:share]
            shares = [piece] + [swap(piece, "row", 2 * j) for j in range(1, chips)]
            shares = shares + [swap(s, "row", 1) for s in shares]
            grad_self, grad_neigh = weight_grads(shares, n_row)

    grad_x = finish(d_pre, w_self, owns, backs)
    return (hidden, grad_x, grad_self, grad_neigh, grad_bias)


def solution(mesh):
    placed = (
        P(("col", "row"), None),
        P(("col", "row")),
        P(("col", "row"), None),
        P(("col", "row"), None, None),
        P(("col", "row")),
        P(("col", "row")),
        P(),
        P(),
        P(),
    )
    return jax.shard_map(
        body,
        mesh=mesh,
        in_specs=placed,
        out_specs=(P(("col", "row"), None), P(("col", "row"), None), P(), P(), P()),
        check_vma=False,
    )
```

```python
import jax
import jax.numpy as jnp
from jax import lax
from jax.experimental import pallas as pl
from jax.experimental.pallas import tpu as pltpu
from jax.sharding import PartitionSpec as P

F32 = jnp.float32
BF16 = jnp.bfloat16
MIB = 1 << 20
RESIDENT_BYTES = 20 * MIB
PARTS = 2
BIAS_ROWS = 16


def vmem():
    return pl.BlockSpec(memory_space=pltpu.VMEM)


def params(limit_mib):
    return pltpu.CompilerParams(vmem_limit_bytes=limit_mib * MIB)


def sds(shape, dtype):
    return jax.ShapeDtypeStruct(shape, dtype)


def densify_far(tile_values, tile_row, tile_col, n_row, n_col, per_dev):
    slots, tile, _ = tile_values.shape
    chips = n_row // 2
    rows = n_row * per_dev
    cols = n_col * per_dev
    cells = rows * cols

    def kernel(row_ref, col_ref, values_ref, dense_ref, table, blank, sem):
        blank[...] = jnp.zeros_like(blank)
        chip = lax.axis_index("row") // 2
        core = lax.axis_index("row") % 2
        col_at = lax.axis_index("col")

        def clear(i, carry):
            for k in range(8):
                table[i * 8 + k] = slots
            return carry

        lax.fori_loop(0, cells // 8, clear, 0)

        def note(i, carry):
            for k in range(4):
                at = i * 4 + k
                table[row_ref[at] * cols + col_ref[at]] = at
            return carry

        lax.fori_loop(0, slots // 4, note, 0)

        def fill(i, carry):
            slot = table[i]
            t = i // cols
            s = i % cols
            owner = t // per_dev
            block = ((owner % 2) ^ core) * chips + ((owner // 2) ^ chip)
            u = (block * per_dev + t % per_dev) * tile
            v = (((s // per_dev) ^ col_at) * per_dev + s % per_dev) * tile
            where = dense_ref.at[
                pl.ds(pl.multiple_of(u, tile), tile), pl.ds(pl.multiple_of(v, tile), tile)
            ]

            @pl.when(slot < slots)
            def _():
                pltpu.make_async_copy(values_ref.at[slot], where, sem).start()

            @pl.when(slot >= slots)
            def _():
                pltpu.make_async_copy(blank, where, sem).start()

            return carry

        lax.fori_loop(0, cells, fill, 0)
        pltpu.make_async_copy(dense_ref, dense_ref, sem).wait()

    shape = (rows * tile, cols * tile)
    return pl.pallas_call(
        kernel,
        out_shape=sds(shape, BF16),
        grid_spec=pltpu.PrefetchScalarGridSpec(
            num_scalar_prefetch=2,
            grid=(),
            in_specs=[pl.BlockSpec(memory_space=pl.ANY)],
            out_specs=pl.BlockSpec(memory_space=pl.ANY),
            scratch_shapes=[
                pltpu.SMEM((cells + cols,), jnp.int32),
                pltpu.VMEM((tile, tile), BF16),
                pltpu.SemaphoreType.DMA,
            ],
        ),
        compiler_params=params(8),
        name="densify_far",
    )(tile_row, tile_col, tile_values)


def densify(tile_values, tile_row, tile_col, features, n_row, n_col, per_dev, wide):
    slots, tile, _ = tile_values.shape
    nodes, width = features.shape
    later = width // wide - 1
    chips = n_row // 2
    rows = n_row * per_dev
    cols = n_col * per_dev
    chip = lax.axis_index("row") // 2
    core = lax.axis_index("row") % 2
    owner = tile_row // per_dev
    block = ((owner % 2) ^ core) * chips + ((owner // 2) ^ chip)
    down = (block * per_dev + tile_row % per_dev) * tile
    down = jnp.where(tile_row < rows, down, rows * tile)
    right = ((tile_col // per_dev) ^ lax.axis_index("col")) * per_dev + tile_col % per_dev
    right = right * tile
    step_slots = 32
    while slots % step_slots:
        step_slots //= 2

    def kernel(down_ref, right_ref, values_ref, feat_ref, dense_ref, *cut_refs):
        step = pl.program_id(0)

        @pl.when(step == 0)
        def _():
            for h in range(later):
                cut_refs[h][...] = feat_ref[:, (h + 1) * wide : (h + 2) * wide]

            def clear(i, carry):
                at = pl.multiple_of(i * tile, tile)
                dense_ref[pl.ds(at, tile), :] = jnp.zeros((tile, cols * tile), BF16)
                return carry

            lax.fori_loop(0, rows, clear, 0)

        for k in range(step_slots):
            u = pl.multiple_of(down_ref[step * step_slots + k], tile)
            v = pl.multiple_of(right_ref[step * step_slots + k], tile)
            dense_ref[pl.ds(u, tile), pl.ds(v, tile)] = values_ref[k]

    res = pl.pallas_call(
        kernel,
        out_shape=[pltpu.VMEM(((rows + 1) * tile, cols * tile), BF16)]
        + [sds((nodes, wide), BF16)] * later,
        grid_spec=pltpu.PrefetchScalarGridSpec(
            num_scalar_prefetch=2,
            grid=(slots // step_slots,),
            in_specs=[
                pl.BlockSpec((step_slots, tile, tile), lambda i, *_: (i, 0, 0)),
                pl.BlockSpec((nodes, width), lambda i, *_: (0, 0)),
            ],
            out_specs=[vmem()] + [pl.BlockSpec((nodes, wide), lambda i, *_: (0, 0))] * later,
        ),
        compiler_params=params(8),
        name="densify",
    )(down, right, pltpu.with_memory_space_constraint(tile_values, pltpu.HBM), features)
    return res[0], res[1:]


def pinned(dense, resident):
    return pltpu.with_memory_space_constraint(dense, pltpu.VMEM) if resident else dense


def forward(dense, pieces, first, count, dtype, resident):
    n_col = len(pieces)
    nodes, wide = pieces[0].shape
    cols = n_col * nodes

    def kernel(*refs):
        dense_ref, piece_refs, out_ref, source = refs[0], refs[1 : 1 + n_col], refs[-2], refs[-1]
        step = pl.program_id(0)

        @pl.when(step == 0)
        def _():
            for m in range(n_col):
                source[m * nodes : (m + 1) * nodes, :] = piece_refs[m][...]

        if resident:
            at = pl.multiple_of((first + step) * nodes, nodes)
            block = dense_ref[pl.ds(at, nodes), :]
        else:
            block = dense_ref[...]
        out_ref[0] = jnp.dot(block, source[...], preferred_element_type=F32).astype(dtype)

    spec = vmem() if resident else pl.BlockSpec((nodes, cols), lambda i: (i + first, 0))
    return pl.pallas_call(
        kernel,
        out_shape=sds((count, nodes, wide), dtype),
        grid=(count,),
        in_specs=[spec] + [pl.BlockSpec((nodes, wide), lambda i: (0, 0))] * n_col,
        out_specs=pl.BlockSpec((1, nodes, wide), lambda i: (i, 0, 0)),
        scratch_shapes=[pltpu.VMEM((cols, wide), BF16)],
        compiler_params=params(8 if resident else 24),
        name="forward",
    )(pinned(dense, resident), *pieces)


def add_parts(keep, got):
    chips, nodes, wide = keep.shape

    def kernel(keep_ref, got_ref, *out_refs):
        for j in range(1, chips):
            out_refs[j - 1][...] = (keep_ref[j] + got_ref[j].astype(F32)).astype(BF16)

    return pl.pallas_call(
        kernel,
        out_shape=[sds((nodes, wide), BF16)] * (chips - 1),
        in_specs=[vmem()] * 2,
        out_specs=[vmem()] * (chips - 1),
        compiler_params=params(8),
        name="add_parts",
    )(keep, got)


def middle(features, degree, cotangent, w_self, w_neigh, bias, parts):
    nodes, width = features.shape
    count = len(parts)
    wide = width // count
    flat = []
    for keep, got, arrivals in parts:
        flat += [keep, got, *arrivals]
    each = len(flat) // count

    def kernel(*refs):
        feat_ref, degree_ref, cot_ref, ws_ref, wn_ref, bias_ref = refs[:6]
        part_refs = refs[6 : 6 + len(flat)]
        hidden_ref, mean_ref, d_pre_ref = refs[6 + len(flat) : 9 + len(flat)]
        d_agg_refs = refs[9 + len(flat) :]
        scale = degree_ref[...].astype(F32)
        scale_down = jnp.transpose(jnp.broadcast_to(scale, (wide, nodes)))
        means = []
        for h in range(count):
            mine = part_refs[h * each : (h + 1) * each]
            total = mine[0][0] + mine[1][0].astype(F32)
            for ref in mine[2:]:
                total = total + ref[...].astype(F32)
            means.append((total / scale_down).astype(BF16))
        neigh_mean = jnp.concatenate(means, axis=1) if count > 1 else means[0]
        mean_ref[...] = neigh_mean
        pre = jnp.dot(feat_ref[...], ws_ref[...], preferred_element_type=F32)
        pre = pre + jnp.dot(neigh_mean, wn_ref[...], preferred_element_type=F32) + bias_ref[...]
        sig = jax.nn.sigmoid(pre)
        hidden_ref[...] = (pre * sig).astype(BF16)
        d_pre = (cot_ref[...].astype(F32) * sig * (1.0 + pre * (1.0 - sig))).astype(BF16)
        d_pre_ref[...] = d_pre
        d_agg = lax.dot_general(
            d_pre, wn_ref[...], (((1,), (1,)), ((), ())), preferred_element_type=F32
        )
        d_agg = (jnp.transpose(d_agg) / scale).astype(BF16)
        for h in range(count):
            d_agg_refs[h][...] = d_agg[h * wide : (h + 1) * wide]

    first_two = [pl.BlockSpec((1, nodes, wide), lambda i: (0, 0, 0))] * 2
    whole = lambda shape: pl.BlockSpec(shape, lambda i: (0,) * len(shape))
    part_specs = (first_two + [whole((nodes, wide))] * (each - 2)) * count
    outs = [sds((nodes, width), BF16)] * 3 + [sds((wide, nodes), BF16)] * count
    args = [features, degree, cotangent, w_self, w_neigh, bias]
    res = pl.pallas_call(
        kernel,
        out_shape=outs,
        grid=(1,),
        in_specs=[whole(a.shape) for a in args] + part_specs,
        out_specs=[whole(o.shape) for o in outs],
        compiler_params=params(12),
        name="middle",
    )(*args, *flat)
    return res[0], res[1], res[2], res[3:]


def local_grads(features, neigh_mean, d_pre, d_agg, n_row):
    nodes, width = features.shape
    wide = d_agg.shape[0]
    chips = n_row // 2
    share = width // n_row

    def kernel(feat_ref, mean_ref, d_pre_ref, d_agg_ref, *refs):
        send_refs, grads_ref = refs[:-1], refs[-1]
        d_pre_now = d_pre_ref[...]
        over = (((0,), (0,)), ((), ()))
        grads_ref[:, 0:width] = lax.dot_general(
            feat_ref[...], d_pre_now, over, preferred_element_type=F32
        )
        grads_ref[:, width:] = lax.dot_general(
            mean_ref[...], d_pre_now, over, preferred_element_type=F32
        )
        bias_sum = jnp.sum(d_pre_now.astype(F32), axis=0, keepdims=True)
        bias_row = jnp.concatenate([bias_sum, bias_sum], axis=1).astype(BF16)
        bias_rows = jnp.broadcast_to(bias_row, (BIAS_ROWS, 2 * width))
        chip = lax.axis_index("row") // 2
        core = lax.axis_index("row") % 2
        for j in range(chips):
            send_refs[j][0:wide, :] = d_agg_ref[...]
            for k in range(2):
                owner = (chip ^ j) * 2 + (core ^ k)
                at = pl.multiple_of(owner * share, share)
                low = wide + k * share
                send_refs[j][low : low + share, :] = grads_ref[pl.ds(at, share), :].astype(BF16)
            send_refs[j][wide + 2 * share :, :] = bias_rows

    return pl.pallas_call(
        kernel,
        out_shape=[sds((wide + 2 * share + BIAS_ROWS, nodes), BF16)] * chips,
        in_specs=[vmem()] * 4,
        out_specs=[vmem()] * chips,
        scratch_shapes=[pltpu.VMEM((width, 2 * width), F32)],
        compiler_params=params(8),
        name="local_grads",
    )(features, neigh_mean, d_pre, d_agg)


def share_partial(pieces, wide, share):
    n_row = len(pieces)
    nodes = pieces[0].shape[1]
    chips = n_row // 2

    def kernel(*refs):
        total_ref, send_ref = refs[-2:]
        total = jnp.zeros((share, nodes), F32)
        bias_total = jnp.zeros((BIAS_ROWS, nodes), F32)
        for b in range(n_row):
            low = wide + (b // chips) * share
            total = total + refs[b][low : low + share, :].astype(F32)
            bias_total = bias_total + refs[b][wide + 2 * share :, :].astype(F32)
        total_ref[0:share, :] = total
        total_ref[share:, :] = bias_total
        send_ref[0:share, :] = total.astype(BF16)
        send_ref[share:, :] = bias_total.astype(BF16)

    return pl.pallas_call(
        kernel,
        out_shape=[sds((share + BIAS_ROWS, nodes), d) for d in (F32, BF16)],
        in_specs=[vmem()] * n_row,
        out_specs=[vmem()] * 2,
        compiler_params=params(8),
        name="share_partial",
    )(*pieces)


def backward(dense, pieces, n_col, wide, resident):
    n_row = len(pieces)
    height, nodes = pieces[0].shape
    rows = n_row * nodes

    def kernel(*refs):
        dense_ref, piece_refs = refs[0], refs[1 : 1 + n_row]
        out_refs = refs[1 + n_row : 1 + n_row + n_col]
        stacked = refs[-1]
        step = pl.program_id(0)

        @pl.when(step == 0)
        def _():
            for b in range(n_row):
                stacked[:, b * nodes : (b + 1) * nodes] = piece_refs[b][0:wide, :]

        for m in range(n_col):

            @pl.when(step == m)
            def _():
                if resident:
                    block = dense_ref[0:rows, m * nodes : (m + 1) * nodes]
                else:
                    block = dense_ref[...]
                out = jnp.dot(stacked[...], block, preferred_element_type=F32)
                out_refs[m][...] = out.astype(out_refs[m].dtype)

    spec = vmem() if resident else pl.BlockSpec((rows, nodes), lambda i: (0, i))
    whole = lambda shape: pl.BlockSpec(shape, lambda i: (0,) * len(shape))
    outs = [sds((wide, nodes), F32)] + [sds((wide, nodes), BF16)] * (n_col - 1)
    res = pl.pallas_call(
        kernel,
        out_shape=outs,
        grid=(n_col,),
        in_specs=[spec] + [whole((height, nodes))] * n_row,
        out_specs=[whole(o.shape) for o in outs],
        scratch_shapes=[pltpu.VMEM((wide, rows), BF16)],
        compiler_params=params(12 if resident else 40),
        name="backward",
    )(pinned(dense, resident), *pieces)
    return res[0], res[1:]


def share_total(total, arrivals):
    height, nodes = total.shape

    def kernel(total_ref, *refs):
        out_ref = refs[-1]
        acc = total_ref[...]
        for ref in refs[:-1]:
            acc = acc + ref[...].astype(F32)
        out_ref[...] = acc

    return pl.pallas_call(
        kernel,
        out_shape=sds((height, nodes), F32),
        in_specs=[vmem()] * (1 + len(arrivals)),
        out_specs=vmem(),
        compiler_params=params(8),
        name="share_total",
    )(total, *arrivals)


def weight_grads(shares, n_row):
    share = shares[0].shape[0]
    width = shares[0].shape[1] // 2
    chips = n_row // 2

    def kernel(*refs):
        self_ref, neigh_ref = refs[-2:]
        chip = lax.axis_index("row") // 2
        core = lax.axis_index("row") % 2
        for b in range(n_row):
            owner = (chip ^ (b % chips)) * 2 + (core ^ (b // chips))
            at = pl.multiple_of(owner * share, share)
            self_ref[pl.ds(at, share), :] = refs[b][:, 0:width]
            neigh_ref[pl.ds(at, share), :] = refs[b][:, width:]

    return pl.pallas_call(
        kernel,
        out_shape=[sds((width, width), F32)] * 2,
        in_specs=[vmem()] * n_row,
        out_specs=[vmem()] * 2,
        compiler_params=params(8),
        name="weight_grads",
    )(*shares)


def finish(d_pre, w_self, owns, arrivals):
    nodes, width = d_pre.shape
    count = len(owns)
    wide = width // count
    others = len(arrivals[0])
    flat = list(owns) + [a for part in arrivals for a in part]

    def kernel(d_pre_ref, ws_ref, *refs):
        out_ref = refs[-1]
        direct = lax.dot_general(
            d_pre_ref[...], ws_ref[...], (((1,), (1,)), ((), ())), preferred_element_type=F32
        )
        for h in range(count):
            acc = refs[h][...]
            for ref in refs[count + h * others : count + (h + 1) * others]:
                acc = acc + ref[...].astype(F32)
            low = h * wide
            out = direct[:, low : low + wide] + jnp.transpose(acc)
            out_ref[:, low : low + wide] = out.astype(BF16)

    return pl.pallas_call(
        kernel,
        out_shape=sds((nodes, width), BF16),
        in_specs=[vmem()] * (2 + len(flat)),
        out_specs=vmem(),
        compiler_params=params(8),
        name="finish",
    )(d_pre, w_self, *flat)


def swap(x, axis, mask):
    size = lax.axis_size(axis)
    return lax.ppermute(x, axis, [(i, i ^ mask) for i in range(size)])


def far_first(n):
    return sorted(range(1, n), key=lambda m: -bin(m).count("1") * n - m)


def body(features, degree, cotangent, tile_values, tile_row, tile_col, w_self, w_neigh, bias):
    nodes, width = features.shape
    tile = tile_values.shape[1]
    n_row = lax.axis_size("row")
    n_col = lax.axis_size("col")
    chips = n_row // 2
    per_dev = nodes // tile
    wide = width // PARTS
    share = width // n_row
    resident = n_row * nodes * n_col * nodes * 2 <= RESIDENT_BYTES

    if resident:
        dense, cuts = densify(
            tile_values, tile_row, tile_col, features, n_row, n_col, per_dev, wide
        )
    else:
        dense = densify_far(tile_values, tile_row, tile_col, n_row, n_col, per_dev)
        cuts = [features[:, h * wide : (h + 1) * wide] for h in range(1, PARTS)]

    parts = []
    for h in range(PARTS):
        own = features[:, 0:wide] if h == 0 else cuts[h - 1]
        pieces = {m: swap(own, "col", m) for m in far_first(n_col)}
        source = [own] + [pieces[m] for m in range(1, n_col)]
        give = forward(dense, source, chips, chips, BF16, resident)
        got = swap(give, "row", 1)
        keep = forward(dense, source, 0, chips, F32, resident)
        sends = add_parts(keep, got)
        arrivals = [swap(sends[j - 1], "row", 2 * j) for j in range(1, chips)]
        parts.append((keep, got, arrivals))

    hidden, neigh_mean, d_pre, d_aggs = middle(
        features, degree[None, :], cotangent, w_self, w_neigh, bias[None, :], parts
    )

    owns, backs = [], []
    for h in range(PARTS):
        last = h == PARTS - 1
        sends = [d_aggs[h]] * chips
        if last:
            sends = local_grads(features, neigh_mean, d_pre, d_aggs[h], n_row)
        if h > 0:
            tied = lax.optimization_barrier((tuple(sends), tuple(mine)))
            sends = tied[0]
        mine = [sends[0]] + [swap(sends[j], "row", 2 * j) for j in range(1, chips)]
        siblings = [swap(piece, "row", 1) for piece in mine]
        pieces = mine + siblings
        own, outs = backward(dense, pieces, n_col, wide, resident)
        arrived = {m: swap(outs[m - 1], "col", m) for m in far_first(n_col)}
        owns.append(own)
        backs.append([arrived[m] for m in range(1, n_col)])
        if last:
            total, send = share_partial(pieces, wide, share)
            summed = share_total(total, [swap(send, "col", m) for m in range(1, n_col)])
            grad_bias = summed[share, 0:width]
            piece = summed[0:share]
            shares = [piece] + [swap(piece, "row", 2 * j) for j in range(1, chips)]
            shares = shares + [swap(part, "row", 1) for part in shares]
            grad_self, grad_neigh = weight_grads(shares, n_row)

    grad_x = finish(d_pre, w_self, owns, backs)
    return (hidden, grad_x, grad_self, grad_neigh, grad_bias)


def solution(mesh):
    placed = (
        P(("col", "row"), None),
        P(("col", "row")),
        P(("col", "row"), None),
        P(("col", "row"), None, None),
        P(("col", "row")),
        P(("col", "row")),
        P(),
        P(),
        P(),
    )
    return jax.shard_map(
        body,
        mesh=mesh,
        in_specs=placed,
        out_specs=(P(("col", "row"), None), P(("col", "row"), None), P(), P(), P()),
        check_vma=False,
    )
```

```python
import jax
import jax.numpy as jnp
from jax import lax
from jax.experimental import pallas as pl
from jax.experimental.pallas import tpu as pltpu
from jax.sharding import PartitionSpec as P

F32 = jnp.float32
BF16 = jnp.bfloat16
MIB = 1 << 20
RESIDENT_BYTES = 20 * MIB
BIAS_ROWS = 16


def vmem():
    return pl.BlockSpec(memory_space=pltpu.VMEM)


def params(limit_mib):
    return pltpu.CompilerParams(vmem_limit_bytes=limit_mib * MIB)


def cost(us):
    return pl.CostEstimate(flops=0, bytes_accessed=int(us * 3.7e6), transcendentals=0)


def sds(shape, dtype):
    return jax.ShapeDtypeStruct(shape, dtype)


def densify_far(tile_values, tile_row, tile_col, n_row, n_col, per_dev):
    slots, tile, _ = tile_values.shape
    chips = n_row // 2
    rows = n_row * per_dev
    cols = n_col * per_dev
    cells = rows * cols

    def kernel(row_ref, col_ref, values_ref, dense_ref, table, blank, sem):
        blank[...] = jnp.zeros_like(blank)
        chip = lax.axis_index("row") // 2
        core = lax.axis_index("row") % 2
        col_at = lax.axis_index("col")

        def clear(i, carry):
            for k in range(8):
                table[i * 8 + k] = slots
            return carry

        lax.fori_loop(0, cells // 8, clear, 0)

        def note(i, carry):
            for k in range(4):
                at = i * 4 + k
                table[row_ref[at] * cols + col_ref[at]] = at
            return carry

        lax.fori_loop(0, slots // 4, note, 0)

        def fill(i, carry):
            slot = table[i]
            t = i // cols
            s = i % cols
            owner = t // per_dev
            block = ((owner % 2) ^ core) * chips + ((owner // 2) ^ chip)
            u = (block * per_dev + t % per_dev) * tile
            v = (((s // per_dev) ^ col_at) * per_dev + s % per_dev) * tile
            where = dense_ref.at[
                pl.ds(pl.multiple_of(u, tile), tile), pl.ds(pl.multiple_of(v, tile), tile)
            ]

            @pl.when(slot < slots)
            def _():
                pltpu.make_async_copy(values_ref.at[slot], where, sem).start()

            @pl.when(slot >= slots)
            def _():
                pltpu.make_async_copy(blank, where, sem).start()

            return carry

        lax.fori_loop(0, cells, fill, 0)
        pltpu.make_async_copy(dense_ref, dense_ref, sem).wait()

    shape = (rows * tile, cols * tile)
    return pl.pallas_call(
        kernel,
        out_shape=sds(shape, BF16),
        grid_spec=pltpu.PrefetchScalarGridSpec(
            num_scalar_prefetch=2,
            grid=(),
            in_specs=[pl.BlockSpec(memory_space=pl.ANY)],
            out_specs=pl.BlockSpec(memory_space=pl.ANY),
            scratch_shapes=[
                pltpu.SMEM((cells + cols,), jnp.int32),
                pltpu.VMEM((tile, tile), BF16),
                pltpu.SemaphoreType.DMA,
            ],
        ),
        compiler_params=params(8),
        cost_estimate=cost(40),
        name="densify_far",
    )(tile_row, tile_col, tile_values)


def densify(tile_values, tile_row, tile_col, n_row, n_col, per_dev):
    slots, tile, _ = tile_values.shape
    chips = n_row // 2
    rows = n_row * per_dev
    cols = n_col * per_dev
    chip = lax.axis_index("row") // 2
    core = lax.axis_index("row") % 2
    owner = tile_row // per_dev
    block = ((owner % 2) ^ core) * chips + ((owner // 2) ^ chip)
    down = (block * per_dev + tile_row % per_dev) * tile
    down = jnp.where(tile_row < rows, down, rows * tile)
    right = ((tile_col // per_dev) ^ lax.axis_index("col")) * per_dev + tile_col % per_dev
    right = right * tile
    step_slots = 32
    while slots % step_slots:
        step_slots //= 2

    def kernel(down_ref, right_ref, values_ref, dense_ref):
        step = pl.program_id(0)

        @pl.when(step == 0)
        def _():
            def clear(i, carry):
                at = pl.multiple_of(i * tile, tile)
                dense_ref[pl.ds(at, tile), :] = jnp.zeros((tile, cols * tile), BF16)
                return carry

            lax.fori_loop(0, rows, clear, 0)

        for k in range(step_slots):
            u = pl.multiple_of(down_ref[step * step_slots + k], tile)
            v = pl.multiple_of(right_ref[step * step_slots + k], tile)
            dense_ref[pl.ds(u, tile), pl.ds(v, tile)] = values_ref[k]

    return pl.pallas_call(
        kernel,
        out_shape=pltpu.VMEM(((rows + 1) * tile, cols * tile), BF16),
        grid_spec=pltpu.PrefetchScalarGridSpec(
            num_scalar_prefetch=2,
            grid=(slots // step_slots,),
            in_specs=[pl.BlockSpec((step_slots, tile, tile), lambda i, *_: (i, 0, 0))],
            out_specs=vmem(),
        ),
        compiler_params=params(8),
        cost_estimate=cost(10),
        name="densify",
    )(down, right, pltpu.with_memory_space_constraint(tile_values, pltpu.HBM))


def pinned(dense, resident):
    return pltpu.with_memory_space_constraint(dense, pltpu.VMEM) if resident else dense


def forward(dense, pieces, first, count, dtype, resident):
    n_col = len(pieces)
    nodes, wide = pieces[0].shape
    cols = n_col * nodes

    def kernel(*refs):
        dense_ref, piece_refs, out_ref, source = refs[0], refs[1 : 1 + n_col], refs[-2], refs[-1]
        step = pl.program_id(0)

        @pl.when(step == 0)
        def _():
            for m in range(n_col):
                source[m * nodes : (m + 1) * nodes, :] = piece_refs[m][...]

        if resident:
            at = pl.multiple_of((first + step) * nodes, nodes)
            block = dense_ref[pl.ds(at, nodes), :]
        else:
            block = dense_ref[...]
        out_ref[0] = jnp.dot(block, source[...], preferred_element_type=F32).astype(dtype)

    spec = vmem() if resident else pl.BlockSpec((nodes, cols), lambda i: (i + first, 0))
    return pl.pallas_call(
        kernel,
        out_shape=sds((count, nodes, wide), dtype),
        grid=(count,),
        in_specs=[spec] + [pl.BlockSpec((nodes, wide), lambda i: (0, 0))] * n_col,
        out_specs=pl.BlockSpec((1, nodes, wide), lambda i: (i, 0, 0)),
        scratch_shapes=[pltpu.VMEM((cols, wide), BF16)],
        compiler_params=params(8 if resident else 24),
        cost_estimate=cost(0.01),
        name="forward",
    )(pinned(dense, resident), *pieces)


def add_parts(keep, got):
    count, nodes, wide = keep.shape

    def kernel(keep_ref, got_ref, *out_refs):
        for j in range(count):
            out_refs[j][...] = (keep_ref[j] + got_ref[j].astype(F32)).astype(BF16)

    return pl.pallas_call(
        kernel,
        out_shape=[sds((nodes, wide), BF16)] * count,
        in_specs=[vmem()] * 2,
        out_specs=[vmem()] * count,
        compiler_params=params(8),
        cost_estimate=cost(0.1),
        name="add_parts",
    )(keep, got)


def middle(features, degree, cotangent, w_self, w_neigh, bias, keep, got, arrivals):
    nodes, width = features.shape

    def kernel(*refs):
        feat_ref, degree_ref, cot_ref, ws_ref, wn_ref, bias_ref = refs[:6]
        keep_ref, got_ref, *part_refs = refs[6:-4]
        hidden_ref, mean_ref, d_pre_ref, d_agg_ref = refs[-4:]
        scale = degree_ref[...].astype(F32)
        scale_down = jnp.transpose(jnp.broadcast_to(scale, (width, nodes)))
        total = keep_ref[0] + got_ref[0].astype(F32)
        for ref in part_refs:
            total = total + ref[...].astype(F32)
        neigh_mean = (total / scale_down).astype(BF16)
        mean_ref[...] = neigh_mean
        pre = jnp.dot(feat_ref[...], ws_ref[...], preferred_element_type=F32)
        pre = pre + jnp.dot(neigh_mean, wn_ref[...], preferred_element_type=F32) + bias_ref[...]
        sig = jax.nn.sigmoid(pre)
        hidden_ref[...] = (pre * sig).astype(BF16)
        d_pre = (cot_ref[...].astype(F32) * sig * (1.0 + pre * (1.0 - sig))).astype(BF16)
        d_pre_ref[...] = d_pre
        d_agg = lax.dot_general(
            d_pre, wn_ref[...], (((1,), (1,)), ((), ())), preferred_element_type=F32
        )
        d_agg_ref[...] = (jnp.transpose(d_agg) / scale).astype(BF16)

    args = [features, degree, cotangent, w_self, w_neigh, bias, keep, got, *arrivals]
    return pl.pallas_call(
        kernel,
        out_shape=[sds((nodes, width), BF16)] * 3 + [sds((width, nodes), BF16)],
        in_specs=[vmem()] * len(args),
        out_specs=[vmem()] * 4,
        compiler_params=params(12),
        cost_estimate=cost(1.5),
        name="middle",
    )(*args)


def local_grads(features, neigh_mean, d_pre, n_row):
    nodes, width = features.shape
    share = width // n_row
    half = width // 2

    def kernel(feat_ref, mean_ref, d_pre_ref, keep_ref, give_ref, grads_ref):
        d_pre_now = d_pre_ref[...]
        over = (((0,), (0,)), ((), ()))
        grads_ref[:, 0:width] = lax.dot_general(
            feat_ref[...], d_pre_now, over, preferred_element_type=F32
        )
        grads_ref[:, width:] = lax.dot_general(
            mean_ref[...], d_pre_now, over, preferred_element_type=F32
        )
        bias_sum = jnp.sum(d_pre_now.astype(F32), axis=0, keepdims=True)
        bias_row = jnp.concatenate([bias_sum, bias_sum], axis=1)
        bias_rows = jnp.broadcast_to(bias_row, (BIAS_ROWS, 2 * width))
        core = lax.axis_index("row") % 2
        for k, ref in enumerate((keep_ref, give_ref)):
            for j in range(n_row // 2):
                at = pl.multiple_of((j * 2 + (core ^ k)) * share, share)
                ref[j * share : (j + 1) * share, :] = grads_ref[pl.ds(at, share), :].astype(ref.dtype)
            ref[half:, :] = bias_rows.astype(ref.dtype)

    return pl.pallas_call(
        kernel,
        out_shape=[sds((half + BIAS_ROWS, 2 * width), d) for d in (F32, BF16)],
        in_specs=[vmem()] * 3,
        out_specs=[vmem()] * 2,
        scratch_shapes=[pltpu.VMEM((width, 2 * width), F32)],
        compiler_params=params(8),
        cost_estimate=cost(0.5),
        name="local_grads",
    )(features, neigh_mean, d_pre)


def column_parts(keep, got, n_col):
    height, columns = keep.shape
    part = (height - BIAS_ROWS) // n_col

    def kernel(keep_ref, got_ref, *refs):
        out_refs, sum_ref = refs[:-1], refs[-1]
        sum_ref[...] = keep_ref[...] + got_ref[...].astype(F32)
        col = lax.axis_index("col")
        for m, ref in enumerate(out_refs):
            at = pl.multiple_of((col ^ m) * part, part)
            ref[0:part, :] = sum_ref[pl.ds(at, part), :].astype(ref.dtype)
            ref[part:, :] = sum_ref[height - BIAS_ROWS :, :].astype(ref.dtype)

    return pl.pallas_call(
        kernel,
        out_shape=[sds((part + BIAS_ROWS, columns), F32 if m == 0 else BF16) for m in range(n_col)],
        in_specs=[vmem()] * 2,
        out_specs=[vmem()] * n_col,
        scratch_shapes=[pltpu.VMEM(keep.shape, F32)],
        compiler_params=params(8),
        cost_estimate=cost(0.1),
        name="column_parts",
    )(keep, got)


def column_sum(own, arrivals):
    height, columns = own.shape
    part = height - BIAS_ROWS

    def kernel(own_ref, *refs):
        send_ref, bias_ref = refs[-2:]
        acc = own_ref[...]
        for ref in refs[:-2]:
            acc = acc + ref[...].astype(F32)
        send_ref[...] = acc[0:part].astype(BF16)
        bias_ref[...] = acc[part:]

    return pl.pallas_call(
        kernel,
        out_shape=[sds((part, columns), BF16), sds((BIAS_ROWS, columns), F32)],
        in_specs=[vmem()] * (1 + len(arrivals)),
        out_specs=[vmem()] * 2,
        compiler_params=params(8),
        cost_estimate=cost(0.1),
        name="column_sum",
    )(own, *arrivals)


def chip_parts(parts, bias_rows, n_row):
    part, columns = parts[0].shape
    n_col = len(parts)
    chips = n_row // 2
    share = part * n_col // chips

    def kernel(*refs):
        part_refs, bias_ref = refs[:n_col], refs[n_col]
        out_refs, whole_ref = refs[n_col + 1 : -1], refs[-1]
        col = lax.axis_index("col")
        for m, ref in enumerate(part_refs):
            at = pl.multiple_of((col ^ m) * part, part)
            whole_ref[pl.ds(at, part), :] = ref[...].astype(F32)
        chip = lax.axis_index("row") // 2
        for j, ref in enumerate(out_refs):
            at = pl.multiple_of((chip ^ j) * share, share)
            ref[0:share, :] = whole_ref[pl.ds(at, share), :]
            ref[share:, :] = bias_ref[...]

    return pl.pallas_call(
        kernel,
        out_shape=[sds((share + BIAS_ROWS, columns), F32)] * chips,
        in_specs=[vmem()] * (n_col + 1),
        out_specs=[vmem()] * chips,
        scratch_shapes=[pltpu.VMEM((part * n_col, columns), F32)],
        compiler_params=params(8),
        cost_estimate=cost(0.1),
        name="chip_parts",
    )(*parts, bias_rows)


def side_by_side(pieces):
    wide, nodes = pieces[0].shape

    def kernel(*refs):
        for j, ref in enumerate(refs[:-1]):
            refs[-1][:, j * nodes : (j + 1) * nodes] = ref[...]

    return pl.pallas_call(
        kernel,
        out_shape=sds((wide, len(pieces) * nodes), BF16),
        in_specs=[vmem()] * len(pieces),
        out_specs=vmem(),
        compiler_params=params(8),
        cost_estimate=cost(0.3),
        name="side_by_side",
    )(*pieces)


def backward(dense, mine, siblings, columns, nodes, resident):
    wide, half = mine.shape
    count = len(columns)
    first = columns[0]

    def kernel(dense_ref, mine_ref, siblings_ref, *out_refs):
        step = pl.program_id(0)
        for i, m in enumerate(columns):

            @pl.when(step == i)
            def _():
                if resident:
                    upper = dense_ref[0:half, m * nodes : (m + 1) * nodes]
                    lower = dense_ref[half : 2 * half, m * nodes : (m + 1) * nodes]
                else:
                    upper = dense_ref[0:half, :]
                    lower = dense_ref[half:, :]
                out = jnp.dot(mine_ref[...], upper, preferred_element_type=F32)
                out = out + jnp.dot(siblings_ref[...], lower, preferred_element_type=F32)
                out_refs[i][...] = out.astype(out_refs[i].dtype)

    spec = vmem() if resident else pl.BlockSpec((2 * half, nodes), lambda i: (0, i + first))
    whole = lambda shape: pl.BlockSpec(shape, lambda i: (0,) * len(shape))
    outs = [sds((wide, nodes), F32 if m == 0 else BF16) for m in columns]
    return pl.pallas_call(
        kernel,
        out_shape=outs,
        grid=(count,),
        in_specs=[spec] + [whole((wide, half))] * 2,
        out_specs=[whole(o.shape) for o in outs],
        compiler_params=params(16 if resident else 48),
        cost_estimate=cost(2.5),
        name="backward",
    )(pinned(dense, resident), mine, siblings)


def share_total(total, arrivals):
    height, columns = total.shape
    share = height - BIAS_ROWS
    width = columns // 2

    def kernel(total_ref, *refs):
        share_ref, bias_ref = refs[-2:]
        acc = total_ref[...]
        for ref in refs[:-2]:
            acc = acc + ref[...].astype(F32)
        share_ref[...] = acc[0:share]
        bias_ref[...] = acc[share : share + 1, 0:width]

    return pl.pallas_call(
        kernel,
        out_shape=[sds((share, columns), F32), sds((1, width), F32)],
        in_specs=[vmem()] * (1 + len(arrivals)),
        out_specs=[vmem()] * 2,
        compiler_params=params(8),
        cost_estimate=cost(0.1),
        name="share_total",
    )(total, *arrivals)


def join(pieces):
    height, columns = pieces[0].shape

    def kernel(*refs):
        for j, ref in enumerate(refs[:-1]):
            refs[-1][j * height : (j + 1) * height, :] = ref[...]

    return pl.pallas_call(
        kernel,
        out_shape=sds((len(pieces) * height, columns), F32),
        in_specs=[vmem()] * len(pieces),
        out_specs=vmem(),
        compiler_params=params(4),
        cost_estimate=cost(0.1),
        name="join",
    )(*pieces)


def weight_grads(mine, siblings, n_row):
    chips = n_row // 2
    share = mine.shape[0] // chips
    width = mine.shape[1] // 2

    def kernel(mine_ref, siblings_ref, self_ref, neigh_ref):
        chip = lax.axis_index("row") // 2
        core = lax.axis_index("row") % 2
        for k, ref in enumerate((mine_ref, siblings_ref)):
            for j in range(chips):
                at = pl.multiple_of(((chip ^ j) * 2 + (core ^ k)) * share, share)
                low = j * share
                self_ref[pl.ds(at, share), :] = ref[low : low + share, 0:width]
                neigh_ref[pl.ds(at, share), :] = ref[low : low + share, width:]

    return pl.pallas_call(
        kernel,
        out_shape=[sds((width, width), F32)] * 2,
        in_specs=[vmem()] * 2,
        out_specs=[vmem()] * 2,
        compiler_params=params(8),
        cost_estimate=cost(1),
        name="weight_grads",
    )(mine, siblings)


def finish(d_pre, w_self, own, arrived):
    nodes, width = d_pre.shape

    def kernel(d_pre_ref, ws_ref, own_ref, *refs):
        out_ref = refs[-1]
        direct = lax.dot_general(
            d_pre_ref[...], ws_ref[...], (((1,), (1,)), ((), ())), preferred_element_type=F32
        )
        acc = own_ref[...]
        for ref in refs[:-1]:
            acc = acc + ref[...].astype(F32)
        out_ref[...] = (direct + jnp.transpose(acc)).astype(BF16)

    return pl.pallas_call(
        kernel,
        out_shape=sds((nodes, width), BF16),
        in_specs=[vmem()] * (3 + len(arrived)),
        out_specs=vmem(),
        compiler_params=params(8),
        cost_estimate=cost(1),
        name="finish",
    )(d_pre, w_self, own, *arrived)


def swap(x, axis, mask):
    size = lax.axis_size(axis)
    return lax.ppermute(x, axis, [(i, i ^ mask) for i in range(size)])


def far_first(n):
    return sorted(range(1, n), key=lambda m: -bin(m).count("1") * n - m)


def body(features, degree, cotangent, tile_values, tile_row, tile_col, w_self, w_neigh, bias):
    nodes, width = features.shape
    tile = tile_values.shape[1]
    n_row = lax.axis_size("row")
    n_col = lax.axis_size("col")
    chips = n_row // 2
    per_dev = nodes // tile
    resident = n_row * nodes * n_col * nodes * 2 <= RESIDENT_BYTES

    arrived = {m: swap(features, "col", m) for m in far_first(n_col)}
    source = [features] + [arrived[m] for m in range(1, n_col)]
    build = densify if resident else densify_far
    dense = build(tile_values, tile_row, tile_col, n_row, n_col, per_dev)

    give = forward(dense, source, chips + 1, chips - 1, BF16, resident)
    got = swap(give, "row", 1)
    keep = forward(dense, source, 1, chips - 1, F32, resident)
    sends = add_parts(keep, got)
    arrivals = [swap(sends[j - 1], "row", 2 * j) for j in range(1, chips)]
    give_own = forward(dense, source, chips, 1, BF16, resident)
    got_own = swap(give_own, "row", 1)
    keep_own = forward(dense, source, 0, 1, F32, resident)
    hidden, neigh_mean, d_pre, d_agg = middle(
        features,
        degree[None, :],
        cotangent,
        w_self,
        w_neigh,
        bias[None, :],
        keep_own,
        got_own,
        arrivals,
    )

    pieces = [d_agg] + [swap(d_agg, "row", 2 * j) for j in range(1, chips)]

    grads_keep, grads_give = local_grads(features, neigh_mean, d_pre, n_row)
    cuts = column_parts(grads_keep, swap(grads_give, "row", 1), n_col)
    part, bias_rows = column_sum(cuts[0], [swap(cuts[m], "col", m) for m in range(1, n_col)])
    pieces, part = lax.optimization_barrier((pieces, part))
    mine = side_by_side(pieces)
    siblings = swap(mine, "row", 1)
    cut = [part] + [swap(part, "col", m) for m in range(1, n_col)]

    near = n_col // 2
    far_outs = backward(dense, mine, siblings, list(range(near, n_col)), nodes, resident)
    mine, siblings, cut, far_outs = lax.optimization_barrier((mine, siblings, cut, far_outs))
    own, *near_outs = backward(dense, mine, siblings, list(range(near)), nodes, resident)
    outs = near_outs + list(far_outs)
    back = {m: swap(outs[m - 1], "col", m) for m in far_first(n_col)}
    back = tuple(back[m] for m in range(1, n_col))

    cuts = chip_parts(cut, bias_rows, n_row)
    arrivals = [swap(cuts[j], "row", 2 * j) for j in range(1, chips)]
    piece, grad_bias = share_total(cuts[0], arrivals)
    shares = join([piece] + [swap(piece, "row", 2 * j) for j in range(1, chips)])
    shares, back = lax.optimization_barrier((shares, back))
    grad_self, grad_neigh = weight_grads(shares, swap(shares, "row", 1), n_row)
    grad_x = finish(d_pre, w_self, own, back)
    return (hidden, grad_x, grad_self, grad_neigh, grad_bias.reshape(width))


def solution(mesh):
    placed = (
        P(("col", "row"), None),
        P(("col", "row")),
        P(("col", "row"), None),
        P(("col", "row"), None, None),
        P(("col", "row")),
        P(("col", "row")),
        P(),
        P(),
        P(),
    )
    return jax.shard_map(
        body,
        mesh=mesh,
        in_specs=placed,
        out_specs=(P(("col", "row"), None), P(("col", "row"), None), P(), P(), P()),
        check_vma=False,
    )
```

```python
import jax
import jax.numpy as jnp
from jax import lax
from jax.experimental import pallas as pl
from jax.experimental.pallas import tpu as pltpu
from jax.sharding import PartitionSpec as P

F32 = jnp.float32
BF16 = jnp.bfloat16
MIB = 1 << 20
RESIDENT_BYTES = 20 * MIB
BIAS_ROWS = 16


def vmem():
    return pl.BlockSpec(memory_space=pltpu.VMEM)


def params(limit_mib):
    return pltpu.CompilerParams(vmem_limit_bytes=limit_mib * MIB)


def cost(us):
    return pl.CostEstimate(flops=0, bytes_accessed=int(us * 3.7e6), transcendentals=0)


def sds(shape, dtype):
    return jax.ShapeDtypeStruct(shape, dtype)


def densify_far(tile_values, tile_row, tile_col, n_row, n_col, per_dev):
    slots, tile, _ = tile_values.shape
    chips = n_row // 2
    rows = n_row * per_dev
    cols = n_col * per_dev
    cells = rows * cols

    def kernel(row_ref, col_ref, values_ref, dense_ref, table, blank, sem):
        blank[...] = jnp.zeros_like(blank)
        chip = lax.axis_index("row") // 2
        core = lax.axis_index("row") % 2
        col_at = lax.axis_index("col")

        def clear(i, carry):
            for k in range(8):
                table[i * 8 + k] = slots
            return carry

        lax.fori_loop(0, cells // 8, clear, 0)

        def note(i, carry):
            for k in range(4):
                at = i * 4 + k
                table[row_ref[at] * cols + col_ref[at]] = at
            return carry

        lax.fori_loop(0, slots // 4, note, 0)

        def fill(i, carry):
            slot = table[i]
            t = i // cols
            s = i % cols
            owner = t // per_dev
            block = ((owner % 2) ^ core) * chips + ((owner // 2) ^ chip)
            u = (block * per_dev + t % per_dev) * tile
            v = (((s // per_dev) ^ col_at) * per_dev + s % per_dev) * tile
            where = dense_ref.at[
                pl.ds(pl.multiple_of(u, tile), tile), pl.ds(pl.multiple_of(v, tile), tile)
            ]

            @pl.when(slot < slots)
            def _():
                pltpu.make_async_copy(values_ref.at[slot], where, sem).start()

            @pl.when(slot >= slots)
            def _():
                pltpu.make_async_copy(blank, where, sem).start()

            return carry

        lax.fori_loop(0, cells, fill, 0)
        pltpu.make_async_copy(dense_ref, dense_ref, sem).wait()

    shape = (rows * tile, cols * tile)
    return pl.pallas_call(
        kernel,
        out_shape=sds(shape, BF16),
        grid_spec=pltpu.PrefetchScalarGridSpec(
            num_scalar_prefetch=2,
            grid=(),
            in_specs=[pl.BlockSpec(memory_space=pl.ANY)],
            out_specs=pl.BlockSpec(memory_space=pl.ANY),
            scratch_shapes=[
                pltpu.SMEM((cells + cols,), jnp.int32),
                pltpu.VMEM((tile, tile), BF16),
                pltpu.SemaphoreType.DMA,
            ],
        ),
        compiler_params=params(8),
        cost_estimate=cost(40),
        name="densify_far",
    )(tile_row, tile_col, tile_values)


def densify(tile_values, tile_row, tile_col, n_row, n_col, per_dev):
    slots, tile, _ = tile_values.shape
    chips = n_row // 2
    rows = n_row * per_dev
    cols = n_col * per_dev
    chip = lax.axis_index("row") // 2
    core = lax.axis_index("row") % 2
    owner = tile_row // per_dev
    block = ((owner % 2) ^ core) * chips + ((owner // 2) ^ chip)
    down = (block * per_dev + tile_row % per_dev) * tile
    down = jnp.where(tile_row < rows, down, rows * tile)
    right = ((tile_col // per_dev) ^ lax.axis_index("col")) * per_dev + tile_col % per_dev
    right = right * tile
    step_slots = 32
    while slots % step_slots:
        step_slots //= 2

    def kernel(down_ref, right_ref, values_ref, dense_ref):
        step = pl.program_id(0)

        @pl.when(step == 0)
        def _():
            def clear(i, carry):
                at = pl.multiple_of(i * tile, tile)
                dense_ref[pl.ds(at, tile), :] = jnp.zeros((tile, cols * tile), BF16)
                return carry

            lax.fori_loop(0, rows, clear, 0)

        for k in range(step_slots):
            u = pl.multiple_of(down_ref[step * step_slots + k], tile)
            v = pl.multiple_of(right_ref[step * step_slots + k], tile)
            dense_ref[pl.ds(u, tile), pl.ds(v, tile)] = values_ref[k]

    return pl.pallas_call(
        kernel,
        out_shape=pltpu.VMEM(((rows + 1) * tile, cols * tile), BF16),
        grid_spec=pltpu.PrefetchScalarGridSpec(
            num_scalar_prefetch=2,
            grid=(slots // step_slots,),
            in_specs=[pl.BlockSpec((step_slots, tile, tile), lambda i, *_: (i, 0, 0))],
            out_specs=vmem(),
        ),
        compiler_params=params(8),
        cost_estimate=cost(10),
        name="densify",
    )(down, right, pltpu.with_memory_space_constraint(tile_values, pltpu.HBM))


def pinned(dense, resident):
    return pltpu.with_memory_space_constraint(dense, pltpu.VMEM) if resident else dense


def forward_early(dense, sources, n_row, resident):
    places = sorted(sources)
    nodes, width = sources[places[0]].shape
    cols = dense.shape[1]

    def kernel(dense_ref, *refs):
        out_ref = refs[-1]
        rows = pl.ds(pl.multiple_of(pl.program_id(0) * nodes, nodes), nodes) if resident else slice(None)
        total = None
        for m, ref in zip(places, refs[:-1]):
            block = dense_ref[rows, m * nodes : (m + 1) * nodes]
            out = jnp.dot(block, ref[...], preferred_element_type=F32)
            total = out if total is None else total + out
        out_ref[0] = total

    spec = vmem() if resident else pl.BlockSpec((nodes, cols), lambda i: (i, 0))
    return pl.pallas_call(
        kernel,
        out_shape=sds((n_row, nodes, width), F32),
        grid=(n_row,),
        in_specs=[spec] + [pl.BlockSpec((nodes, width), lambda i: (0, 0))] * len(places),
        out_specs=pl.BlockSpec((1, nodes, width), lambda i: (i, 0, 0)),
        compiler_params=params(8 if resident else 32),
        cost_estimate=cost(5),
        name="forward_early",
    )(pinned(dense, resident), *[sources[m] for m in places])


def forward_late(dense, early, place, piece, first, count, dtype, resident):
    nodes, width = piece.shape

    def kernel(dense_ref, early_ref, piece_ref, out_ref):
        if resident:
            at = pl.multiple_of((first + pl.program_id(0)) * nodes, nodes)
            block = dense_ref[pl.ds(at, nodes), place * nodes : (place + 1) * nodes]
        else:
            block = dense_ref[...]
        out = jnp.dot(block, piece_ref[...], preferred_element_type=F32)
        out_ref[0] = (early_ref[0] + out).astype(dtype)

    spec = vmem() if resident else pl.BlockSpec((nodes, nodes), lambda i: (i + first, place))
    return pl.pallas_call(
        kernel,
        out_shape=sds((count, nodes, width), dtype),
        grid=(count,),
        in_specs=[
            spec,
            pl.BlockSpec((1, nodes, width), lambda i: (i + first, 0, 0)),
            pl.BlockSpec((nodes, width), lambda i: (0, 0)),
        ],
        out_specs=pl.BlockSpec((1, nodes, width), lambda i: (i, 0, 0)),
        compiler_params=params(8),
        cost_estimate=cost(1),
        name="forward_late",
    )(pinned(dense, resident), early, piece)


def add_parts(keep, got):
    count, nodes, wide = keep.shape

    def kernel(keep_ref, got_ref, *out_refs):
        for j in range(count):
            out_refs[j][...] = (keep_ref[j] + got_ref[j].astype(F32)).astype(BF16)

    return pl.pallas_call(
        kernel,
        out_shape=[sds((nodes, wide), BF16)] * count,
        in_specs=[vmem()] * 2,
        out_specs=[vmem()] * count,
        compiler_params=params(8),
        cost_estimate=cost(0.1),
        name="add_parts",
    )(keep, got)


def middle(features, degree, cotangent, w_self, w_neigh, bias, keep, got, arrivals):
    nodes, width = features.shape

    def kernel(*refs):
        feat_ref, degree_ref, cot_ref, ws_ref, wn_ref, bias_ref = refs[:6]
        keep_ref, got_ref, *part_refs = refs[6:-4]
        hidden_ref, mean_ref, d_pre_ref, d_agg_ref = refs[-4:]
        scale = degree_ref[...].astype(F32)
        scale_down = jnp.transpose(jnp.broadcast_to(scale, (width, nodes)))
        total = keep_ref[0] + got_ref[0].astype(F32)
        for ref in part_refs:
            total = total + ref[...].astype(F32)
        neigh_mean = (total / scale_down).astype(BF16)
        mean_ref[...] = neigh_mean
        pre = jnp.dot(feat_ref[...], ws_ref[...], preferred_element_type=F32)
        pre = pre + jnp.dot(neigh_mean, wn_ref[...], preferred_element_type=F32) + bias_ref[...]
        sig = jax.nn.sigmoid(pre)
        hidden_ref[...] = (pre * sig).astype(BF16)
        d_pre = (cot_ref[...].astype(F32) * sig * (1.0 + pre * (1.0 - sig))).astype(BF16)
        d_pre_ref[...] = d_pre
        d_agg = lax.dot_general(
            d_pre, wn_ref[...], (((1,), (1,)), ((), ())), preferred_element_type=F32
        )
        d_agg_ref[...] = (jnp.transpose(d_agg) / scale).astype(BF16)

    args = [features, degree, cotangent, w_self, w_neigh, bias, keep, got, *arrivals]
    return pl.pallas_call(
        kernel,
        out_shape=[sds((nodes, width), BF16)] * 3 + [sds((width, nodes), BF16)],
        in_specs=[vmem()] * len(args),
        out_specs=[vmem()] * 4,
        compiler_params=params(12),
        cost_estimate=cost(1.5),
        name="middle",
    )(*args)


def local_grads(features, neigh_mean, d_pre, n_row):
    nodes, width = features.shape
    share = width // n_row
    half = width // 2

    def kernel(feat_ref, mean_ref, d_pre_ref, keep_ref, give_ref, grads_ref):
        d_pre_now = d_pre_ref[...]
        over = (((0,), (0,)), ((), ()))
        grads_ref[:, 0:width] = lax.dot_general(
            feat_ref[...], d_pre_now, over, preferred_element_type=F32
        )
        grads_ref[:, width:] = lax.dot_general(
            mean_ref[...], d_pre_now, over, preferred_element_type=F32
        )
        bias_sum = jnp.sum(d_pre_now.astype(F32), axis=0, keepdims=True)
        bias_row = jnp.concatenate([bias_sum, bias_sum], axis=1)
        bias_rows = jnp.broadcast_to(bias_row, (BIAS_ROWS, 2 * width))
        core = lax.axis_index("row") % 2
        for k, ref in enumerate((keep_ref, give_ref)):
            for j in range(n_row // 2):
                at = pl.multiple_of((j * 2 + (core ^ k)) * share, share)
                ref[j * share : (j + 1) * share, :] = grads_ref[pl.ds(at, share), :].astype(ref.dtype)
            ref[half:, :] = bias_rows.astype(BF16).astype(ref.dtype)

    return pl.pallas_call(
        kernel,
        out_shape=[sds((half + BIAS_ROWS, 2 * width), d) for d in (F32, BF16)],
        in_specs=[vmem()] * 3,
        out_specs=[vmem()] * 2,
        scratch_shapes=[pltpu.VMEM((width, 2 * width), F32)],
        compiler_params=params(8),
        cost_estimate=cost(0.5),
        name="local_grads",
    )(features, neigh_mean, d_pre)


def add_sent(keep, got, kind):
    def kernel(keep_ref, got_ref, out_ref):
        out_ref[...] = (keep_ref[...].astype(F32) + got_ref[...].astype(F32)).astype(kind)

    return pl.pallas_call(
        kernel,
        out_shape=sds(keep.shape, kind),
        in_specs=[vmem()] * 2,
        out_specs=vmem(),
        compiler_params=params(8),
        cost_estimate=cost(0.1),
        name="add_sent",
    )(keep, got)


def chip_parts(half, n_row):
    height, columns = half.shape
    rows = height - BIAS_ROWS
    chips = n_row // 2
    share = rows // chips

    def kernel(half_ref, *out_refs):
        chip = lax.axis_index("row") // 2
        for j, ref in enumerate(out_refs):
            at = pl.multiple_of((chip ^ j) * share, share)
            ref[0:share, :] = half_ref[pl.ds(at, share), :]
            ref[share:, :] = half_ref[rows:, :]

    return pl.pallas_call(
        kernel,
        out_shape=[sds((share + BIAS_ROWS, columns), F32)] * chips,
        in_specs=[vmem()],
        out_specs=[vmem()] * chips,
        compiler_params=params(8),
        cost_estimate=cost(0.1),
        name="chip_parts",
    )(half)


def side_by_side(pieces):
    wide, nodes = pieces[0].shape

    def kernel(*refs):
        for j, ref in enumerate(refs[:-1]):
            refs[-1][:, j * nodes : (j + 1) * nodes] = ref[...]

    return pl.pallas_call(
        kernel,
        out_shape=sds((wide, len(pieces) * nodes), BF16),
        in_specs=[vmem()] * len(pieces),
        out_specs=vmem(),
        compiler_params=params(8),
        cost_estimate=cost(0.3),
        name="side_by_side",
    )(*pieces)


def backward_early(dense, mine, n_col, nodes, resident):
    wide, half = mine.shape

    def kernel(dense_ref, mine_ref, out_ref):
        if resident:
            at = pl.multiple_of(pl.program_id(0) * nodes, nodes)
            block = dense_ref[0:half, pl.ds(at, nodes)]
        else:
            block = dense_ref[...]
        out_ref[0] = jnp.dot(mine_ref[...], block, preferred_element_type=F32)

    spec = vmem() if resident else pl.BlockSpec((half, nodes), lambda i: (0, i))
    return pl.pallas_call(
        kernel,
        out_shape=sds((n_col, wide, nodes), F32),
        grid=(n_col,),
        in_specs=[spec, pl.BlockSpec((wide, half), lambda i: (0, 0))],
        out_specs=pl.BlockSpec((1, wide, nodes), lambda i: (i, 0, 0)),
        compiler_params=params(8 if resident else 24),
        cost_estimate=cost(2.5),
        name="backward_early",
    )(pinned(dense, resident), mine)


def backward_late(dense, early, siblings, n_col, nodes, resident):
    wide, half = siblings.shape

    def kernel(dense_ref, early_ref, siblings_ref, *out_refs):
        step = pl.program_id(0)
        for m in range(n_col):

            @pl.when(step == m)
            def _():
                if resident:
                    block = dense_ref[half : 2 * half, m * nodes : (m + 1) * nodes]
                else:
                    block = dense_ref[...]
                out = jnp.dot(siblings_ref[...], block, preferred_element_type=F32)
                out_refs[m][...] = (early_ref[0] + out).astype(out_refs[m].dtype)

    spec = vmem() if resident else pl.BlockSpec((half, nodes), lambda i: (1, i))
    whole = lambda shape: pl.BlockSpec(shape, lambda i: (0,) * len(shape))
    outs = [sds((wide, nodes), F32 if m == 0 else BF16) for m in range(n_col)]
    return pl.pallas_call(
        kernel,
        out_shape=outs,
        grid=(n_col,),
        in_specs=[spec, pl.BlockSpec((1, wide, nodes), lambda i: (i, 0, 0)), whole((wide, half))],
        out_specs=[whole(o.shape) for o in outs],
        compiler_params=params(10 if resident else 32),
        cost_estimate=cost(2.5),
        name="backward_late",
    )(pinned(dense, resident), early, siblings)


def share_total(pieces):
    height, columns = pieces[0].shape
    share = height - BIAS_ROWS
    width = columns // 2

    def kernel(*refs):
        share_ref, bias_ref = refs[-2:]
        terms = [ref[...] for ref in refs[:-2]]
        while len(terms) > 1:
            terms = [terms[i] + terms[i + 1] for i in range(0, len(terms), 2)]
        share_ref[...] = terms[0][0:share]
        bias_ref[...] = terms[0][share : share + 1, 0:width]

    return pl.pallas_call(
        kernel,
        out_shape=[sds((share, columns), F32), sds((1, width), F32)],
        in_specs=[vmem()] * len(pieces),
        out_specs=[vmem()] * 2,
        compiler_params=params(8),
        cost_estimate=cost(0.1),
        name="share_total",
    )(*pieces)


def join(pieces):
    height, columns = pieces[0].shape

    def kernel(*refs):
        for j, ref in enumerate(refs[:-1]):
            refs[-1][j * height : (j + 1) * height, :] = ref[...]

    return pl.pallas_call(
        kernel,
        out_shape=sds((len(pieces) * height, columns), F32),
        in_specs=[vmem()] * len(pieces),
        out_specs=vmem(),
        compiler_params=params(4),
        cost_estimate=cost(0.1),
        name="join",
    )(*pieces)


def weight_grads(mine, siblings, n_row):
    chips = n_row // 2
    share = mine.shape[0] // chips
    width = mine.shape[1] // 2

    def kernel(mine_ref, siblings_ref, self_ref, neigh_ref):
        chip = lax.axis_index("row") // 2
        core = lax.axis_index("row") % 2
        for k, ref in enumerate((mine_ref, siblings_ref)):
            for j in range(chips):
                at = pl.multiple_of(((chip ^ j) * 2 + (core ^ k)) * share, share)
                low = j * share
                self_ref[pl.ds(at, share), :] = ref[low : low + share, 0:width]
                neigh_ref[pl.ds(at, share), :] = ref[low : low + share, width:]

    return pl.pallas_call(
        kernel,
        out_shape=[sds((width, width), F32)] * 2,
        in_specs=[vmem()] * 2,
        out_specs=[vmem()] * 2,
        compiler_params=params(8),
        cost_estimate=cost(1),
        name="weight_grads",
    )(mine, siblings)


def finish(d_pre, w_self, own, arrived):
    nodes, width = d_pre.shape

    def kernel(d_pre_ref, ws_ref, own_ref, *refs):
        out_ref = refs[-1]
        direct = lax.dot_general(
            d_pre_ref[...], ws_ref[...], (((1,), (1,)), ((), ())), preferred_element_type=F32
        )
        acc = own_ref[...]
        for ref in refs[:-1]:
            acc = acc + ref[...].astype(F32)
        out_ref[...] = (direct + jnp.transpose(acc)).astype(BF16)

    return pl.pallas_call(
        kernel,
        out_shape=sds((nodes, width), BF16),
        in_specs=[vmem()] * (3 + len(arrived)),
        out_specs=vmem(),
        compiler_params=params(8),
        cost_estimate=cost(1),
        name="finish",
    )(d_pre, w_self, own, *arrived)


def swap(x, axis, mask):
    size = lax.axis_size(axis)
    return lax.ppermute(x, axis, [(i, i ^ mask) for i in range(size)])


def far_first(n):
    return sorted(range(1, n), key=lambda m: -bin(m).count("1") * n - m)


def body(features, degree, cotangent, tile_values, tile_row, tile_col, w_self, w_neigh, bias):
    nodes, width = features.shape
    tile = tile_values.shape[1]
    n_row = lax.axis_size("row")
    n_col = lax.axis_size("col")
    chips = n_row // 2
    per_dev = nodes // tile
    resident = n_row * nodes * n_col * nodes * 2 <= RESIDENT_BYTES

    source = {m: swap(features, "col", m) for m in far_first(n_col)}
    source[0] = features
    build = densify if resident else densify_far
    dense = build(tile_values, tile_row, tile_col, n_row, n_col, per_dev)

    last = n_col // 2
    last_piece = source.pop(last)
    early = forward_early(dense, source, n_row, resident)

    def late(first, count, dtype):
        return forward_late(dense, early, last, last_piece, first, count, dtype, resident)

    give = late(chips + 1, chips - 1, BF16)
    got = swap(give, "row", 1)
    keep = late(1, chips - 1, F32)
    sends = add_parts(keep, got)
    arrivals = [swap(sends[j - 1], "row", 2 * j) for j in range(1, chips)]
    give_own = late(chips, 1, BF16)
    got_own = swap(give_own, "row", 1)
    keep_own = late(0, 1, F32)
    hidden, neigh_mean, d_pre, d_agg = middle(
        features,
        degree[None, :],
        cotangent,
        w_self,
        w_neigh,
        bias[None, :],
        keep_own,
        got_own,
        arrivals,
    )

    pieces = [d_agg] + [swap(d_agg, "row", 2 * j) for j in range(1, chips)]

    kept, sent = local_grads(features, neigh_mean, d_pre, n_row)
    total = add_sent(kept, swap(sent, "row", 1), BF16)
    mask = n_col // 2
    while mask > 1:
        total = add_sent(total, swap(total, "col", mask), BF16)
        mask //= 2
    pieces, total = lax.optimization_barrier((pieces, total))
    mine = side_by_side(pieces)
    siblings = swap(mine, "row", 1)
    got_last = swap(total, "col", 1)

    early = backward_early(dense, mine, n_col, nodes, resident)
    own, *outs = backward_late(dense, early, siblings, n_col, nodes, resident)
    back = {m: swap(outs[m - 1], "col", m) for m in far_first(n_col)}
    back = tuple(back[m] for m in range(1, n_col))

    got_last, _ = lax.optimization_barrier((got_last, outs))
    cuts = chip_parts(add_sent(total, got_last, F32), n_row)
    arrivals = [swap(cuts[j], "row", 2 * j) for j in range(1, chips)]
    piece, grad_bias = share_total([cuts[0]] + arrivals)
    shares = join([piece] + [swap(piece, "row", 2 * j) for j in range(1, chips)])
    shares, back = lax.optimization_barrier((shares, back))
    grad_self, grad_neigh = weight_grads(shares, swap(shares, "row", 1), n_row)
    grad_x = finish(d_pre, w_self, own, back)
    return (hidden, grad_x, grad_self, grad_neigh, grad_bias.reshape(width))


def solution(mesh):
    placed = (
        P(("col", "row"), None),
        P(("col", "row")),
        P(("col", "row"), None),
        P(("col", "row"), None, None),
        P(("col", "row")),
        P(("col", "row")),
        P(),
        P(),
        P(),
    )
    return jax.shard_map(
        body,
        mesh=mesh,
        in_specs=placed,
        out_specs=(P(("col", "row"), None), P(("col", "row"), None), P(), P(), P()),
        check_vma=False,
    )
```

```python
import jax
import jax.numpy as jnp
from jax import lax
from jax.experimental import pallas as pl
from jax.experimental.pallas import tpu as pltpu
from jax.sharding import PartitionSpec as P

F32 = jnp.float32
BF16 = jnp.bfloat16
MIB = 1 << 20
RESIDENT_BYTES = 20 * MIB
BIAS_ROWS = 16


def vmem():
    return pl.BlockSpec(memory_space=pltpu.VMEM)


def params(limit_mib):
    return pltpu.CompilerParams(vmem_limit_bytes=limit_mib * MIB)


def cost(us):
    return pl.CostEstimate(flops=0, bytes_accessed=int(us * 3.7e6), transcendentals=0)


def sds(shape, dtype):
    return jax.ShapeDtypeStruct(shape, dtype)


def densify_far(tile_values, tile_row, tile_col, n_row, n_col, per_dev):
    slots, tile, _ = tile_values.shape
    chips = n_row // 2
    rows = n_row * per_dev
    cols = n_col * per_dev
    cells = rows * cols

    def kernel(row_ref, col_ref, values_ref, dense_ref, table, blank, sem):
        blank[...] = jnp.zeros_like(blank)
        chip = lax.axis_index("row") // 2
        core = lax.axis_index("row") % 2
        col_at = lax.axis_index("col")

        def clear(i, carry):
            for k in range(8):
                table[i * 8 + k] = slots
            return carry

        lax.fori_loop(0, cells // 8, clear, 0)

        def note(i, carry):
            for k in range(4):
                at = i * 4 + k
                table[row_ref[at] * cols + col_ref[at]] = at
            return carry

        lax.fori_loop(0, slots // 4, note, 0)

        def fill(i, carry):
            slot = table[i]
            t = i // cols
            s = i % cols
            owner = t // per_dev
            block = ((owner % 2) ^ core) * chips + ((owner // 2) ^ chip)
            u = (block * per_dev + t % per_dev) * tile
            v = (((s // per_dev) ^ col_at) * per_dev + s % per_dev) * tile
            where = dense_ref.at[
                pl.ds(pl.multiple_of(u, tile), tile), pl.ds(pl.multiple_of(v, tile), tile)
            ]

            @pl.when(slot < slots)
            def _():
                pltpu.make_async_copy(values_ref.at[slot], where, sem).start()

            @pl.when(slot >= slots)
            def _():
                pltpu.make_async_copy(blank, where, sem).start()

            return carry

        lax.fori_loop(0, cells, fill, 0)
        pltpu.make_async_copy(dense_ref, dense_ref, sem).wait()

    shape = (rows * tile, cols * tile)
    return pl.pallas_call(
        kernel,
        out_shape=sds(shape, BF16),
        grid_spec=pltpu.PrefetchScalarGridSpec(
            num_scalar_prefetch=2,
            grid=(),
            in_specs=[pl.BlockSpec(memory_space=pl.ANY)],
            out_specs=pl.BlockSpec(memory_space=pl.ANY),
            scratch_shapes=[
                pltpu.SMEM((cells + cols,), jnp.int32),
                pltpu.VMEM((tile, tile), BF16),
                pltpu.SemaphoreType.DMA,
            ],
        ),
        compiler_params=params(8),
        cost_estimate=cost(40),
        name="densify_far",
    )(tile_row, tile_col, tile_values)


def densify(tile_values, tile_row, tile_col, n_row, n_col, per_dev):
    slots, tile, _ = tile_values.shape
    chips = n_row // 2
    rows = n_row * per_dev
    cols = n_col * per_dev
    chip = lax.axis_index("row") // 2
    core = lax.axis_index("row") % 2
    owner = tile_row // per_dev
    block = ((owner % 2) ^ core) * chips + ((owner // 2) ^ chip)
    down = (block * per_dev + tile_row % per_dev) * tile
    down = jnp.where(tile_row < rows, down, rows * tile)
    right = ((tile_col // per_dev) ^ lax.axis_index("col")) * per_dev + tile_col % per_dev
    right = right * tile
    step_slots = 32
    while slots % step_slots:
        step_slots //= 2

    def kernel(down_ref, right_ref, values_ref, dense_ref):
        step = pl.program_id(0)

        @pl.when(step == 0)
        def _():
            def clear(i, carry):
                at = pl.multiple_of(i * tile, tile)
                dense_ref[pl.ds(at, tile), :] = jnp.zeros((tile, cols * tile), BF16)
                return carry

            lax.fori_loop(0, rows, clear, 0)

        for k in range(step_slots):
            u = pl.multiple_of(down_ref[step * step_slots + k], tile)
            v = pl.multiple_of(right_ref[step * step_slots + k], tile)
            dense_ref[pl.ds(u, tile), pl.ds(v, tile)] = values_ref[k]

    return pl.pallas_call(
        kernel,
        out_shape=pltpu.VMEM(((rows + 1) * tile, cols * tile), BF16),
        grid_spec=pltpu.PrefetchScalarGridSpec(
            num_scalar_prefetch=2,
            grid=(slots // step_slots,),
            in_specs=[pl.BlockSpec((step_slots, tile, tile), lambda i, *_: (i, 0, 0))],
            out_specs=vmem(),
        ),
        compiler_params=params(8),
        cost_estimate=cost(10),
        name="densify",
    )(down, right, pltpu.with_memory_space_constraint(tile_values, pltpu.HBM))


def pinned(dense, resident):
    return pltpu.with_memory_space_constraint(dense, pltpu.VMEM) if resident else dense


def forward_early(dense, sources, n_row, resident):
    places = sorted(sources)
    nodes, width = sources[places[0]].shape
    cols = dense.shape[1]

    def kernel(dense_ref, *refs):
        out_ref = refs[-1]
        rows = pl.ds(pl.multiple_of(pl.program_id(0) * nodes, nodes), nodes) if resident else slice(None)
        total = None
        for m, ref in zip(places, refs[:-1]):
            block = dense_ref[rows, m * nodes : (m + 1) * nodes]
            out = jnp.dot(block, ref[...], preferred_element_type=F32)
            total = out if total is None else total + out
        out_ref[0] = total

    spec = vmem() if resident else pl.BlockSpec((nodes, cols), lambda i: (i, 0))
    return pl.pallas_call(
        kernel,
        out_shape=sds((n_row, nodes, width), F32),
        grid=(n_row,),
        in_specs=[spec] + [pl.BlockSpec((nodes, width), lambda i: (0, 0))] * len(places),
        out_specs=pl.BlockSpec((1, nodes, width), lambda i: (i, 0, 0)),
        compiler_params=params(8 if resident else 32),
        cost_estimate=cost(5),
        name="forward_early",
    )(pinned(dense, resident), *[sources[m] for m in places])


def forward_late(dense, early, place, piece, first, count, dtype, resident):
    nodes, width = piece.shape

    def kernel(dense_ref, early_ref, piece_ref, out_ref):
        if resident:
            at = pl.multiple_of((first + pl.program_id(0)) * nodes, nodes)
            block = dense_ref[pl.ds(at, nodes), place * nodes : (place + 1) * nodes]
        else:
            block = dense_ref[...]
        out = jnp.dot(block, piece_ref[...], preferred_element_type=F32)
        out_ref[0] = (early_ref[0] + out).astype(dtype)

    spec = vmem() if resident else pl.BlockSpec((nodes, nodes), lambda i: (i + first, place))
    return pl.pallas_call(
        kernel,
        out_shape=sds((count, nodes, width), dtype),
        grid=(count,),
        in_specs=[
            spec,
            pl.BlockSpec((1, nodes, width), lambda i: (i + first, 0, 0)),
            pl.BlockSpec((nodes, width), lambda i: (0, 0)),
        ],
        out_specs=pl.BlockSpec((1, nodes, width), lambda i: (i, 0, 0)),
        compiler_params=params(8),
        cost_estimate=cost(1),
        name="forward_late",
    )(pinned(dense, resident), early, piece)


def add_parts(keep, got):
    count, nodes, wide = keep.shape

    def kernel(keep_ref, got_ref, *out_refs):
        for j in range(count):
            out_refs[j][...] = (keep_ref[j] + got_ref[j].astype(F32)).astype(BF16)

    return pl.pallas_call(
        kernel,
        out_shape=[sds((nodes, wide), BF16)] * count,
        in_specs=[vmem()] * 2,
        out_specs=[vmem()] * count,
        compiler_params=params(8),
        cost_estimate=cost(0.1),
        name="add_parts",
    )(keep, got)


def middle(features, degree, cotangent, w_self, w_neigh, bias, keep, got, arrivals):
    nodes, width = features.shape

    def kernel(*refs):
        feat_ref, degree_ref, cot_ref, ws_ref, wn_ref, bias_ref = refs[:6]
        keep_ref, got_ref, *part_refs = refs[6:-4]
        hidden_ref, mean_ref, d_pre_ref, d_agg_ref = refs[-4:]
        scale = degree_ref[...].astype(F32)
        scale_down = jnp.transpose(jnp.broadcast_to(scale, (width, nodes)))
        total = keep_ref[0] + got_ref[0].astype(F32)
        for ref in part_refs:
            total = total + ref[...].astype(F32)
        neigh_mean = (total / scale_down).astype(BF16)
        mean_ref[...] = neigh_mean
        pre = jnp.dot(feat_ref[...], ws_ref[...], preferred_element_type=F32)
        pre = pre + jnp.dot(neigh_mean, wn_ref[...], preferred_element_type=F32) + bias_ref[...]
        sig = jax.nn.sigmoid(pre)
        hidden_ref[...] = (pre * sig).astype(BF16)
        d_pre = (cot_ref[...].astype(F32) * sig * (1.0 + pre * (1.0 - sig))).astype(BF16)
        d_pre_ref[...] = d_pre
        d_agg = lax.dot_general(
            d_pre, wn_ref[...], (((1,), (1,)), ((), ())), preferred_element_type=F32
        )
        d_agg_ref[...] = (jnp.transpose(d_agg) / scale).astype(BF16)

    args = [features, degree, cotangent, w_self, w_neigh, bias, keep, got, *arrivals]
    return pl.pallas_call(
        kernel,
        out_shape=[sds((nodes, width), BF16)] * 3 + [sds((width, nodes), BF16)],
        in_specs=[vmem()] * len(args),
        out_specs=[vmem()] * 4,
        compiler_params=params(12),
        cost_estimate=cost(1.5),
        name="middle",
    )(*args)


def local_grads(features, neigh_mean, d_pre, n_row):
    nodes, width = features.shape
    share = width // n_row
    half = width // 2

    def kernel(feat_ref, mean_ref, d_pre_ref, keep_ref, give_ref, grads_ref):
        d_pre_now = d_pre_ref[...]
        over = (((0,), (0,)), ((), ()))
        grads_ref[:, 0:width] = lax.dot_general(
            feat_ref[...], d_pre_now, over, preferred_element_type=F32
        )
        grads_ref[:, width:] = lax.dot_general(
            mean_ref[...], d_pre_now, over, preferred_element_type=F32
        )
        bias_sum = jnp.sum(d_pre_now.astype(F32), axis=0, keepdims=True)
        bias_row = jnp.concatenate([bias_sum, bias_sum], axis=1)
        bias_rows = jnp.broadcast_to(bias_row, (BIAS_ROWS, 2 * width))
        core = lax.axis_index("row") % 2
        for k, ref in enumerate((keep_ref, give_ref)):
            for j in range(n_row // 2):
                at = pl.multiple_of((j * 2 + (core ^ k)) * share, share)
                ref[j * share : (j + 1) * share, :] = grads_ref[pl.ds(at, share), :].astype(ref.dtype)
            ref[half:, :] = bias_rows.astype(BF16).astype(ref.dtype)

    return pl.pallas_call(
        kernel,
        out_shape=[sds((half + BIAS_ROWS, 2 * width), d) for d in (F32, BF16)],
        in_specs=[vmem()] * 3,
        out_specs=[vmem()] * 2,
        scratch_shapes=[pltpu.VMEM((width, 2 * width), F32)],
        compiler_params=params(8),
        cost_estimate=cost(0.5),
        name="local_grads",
    )(features, neigh_mean, d_pre)


def add_sent(keep, got, kind):
    def kernel(keep_ref, got_ref, out_ref):
        out_ref[...] = (keep_ref[...].astype(F32) + got_ref[...].astype(F32)).astype(kind)

    return pl.pallas_call(
        kernel,
        out_shape=sds(keep.shape, kind),
        in_specs=[vmem()] * 2,
        out_specs=vmem(),
        compiler_params=params(8),
        cost_estimate=cost(0.1),
        name="add_sent",
    )(keep, got)


def chip_parts(half, n_row):
    height, columns = half.shape
    rows = height - BIAS_ROWS
    chips = n_row // 2
    share = rows // chips

    def kernel(half_ref, *out_refs):
        chip = lax.axis_index("row") // 2
        for j, ref in enumerate(out_refs):
            at = pl.multiple_of((chip ^ j) * share, share)
            ref[0:share, :] = half_ref[pl.ds(at, share), :]
            ref[share:, :] = half_ref[rows:, :]

    return pl.pallas_call(
        kernel,
        out_shape=[sds((share + BIAS_ROWS, columns), F32)] * chips,
        in_specs=[vmem()],
        out_specs=[vmem()] * chips,
        compiler_params=params(8),
        cost_estimate=cost(0.1),
        name="chip_parts",
    )(half)


def side_by_side(pieces):
    wide, nodes = pieces[0].shape

    def kernel(*refs):
        for j, ref in enumerate(refs[:-1]):
            refs[-1][:, j * nodes : (j + 1) * nodes] = ref[...]

    return pl.pallas_call(
        kernel,
        out_shape=sds((wide, len(pieces) * nodes), BF16),
        in_specs=[vmem()] * len(pieces),
        out_specs=vmem(),
        compiler_params=params(8),
        cost_estimate=cost(0.3),
        name="side_by_side",
    )(*pieces)


def backward_early(dense, mine, n_col, nodes, resident):
    wide, half = mine.shape

    def kernel(dense_ref, mine_ref, out_ref):
        if resident:
            at = pl.multiple_of(pl.program_id(0) * nodes, nodes)
            block = dense_ref[0:half, pl.ds(at, nodes)]
        else:
            block = dense_ref[...]
        out_ref[0] = jnp.dot(mine_ref[...], block, preferred_element_type=F32)

    spec = vmem() if resident else pl.BlockSpec((half, nodes), lambda i: (0, i))
    return pl.pallas_call(
        kernel,
        out_shape=sds((n_col, wide, nodes), F32),
        grid=(n_col,),
        in_specs=[spec, pl.BlockSpec((wide, half), lambda i: (0, 0))],
        out_specs=pl.BlockSpec((1, wide, nodes), lambda i: (i, 0, 0)),
        compiler_params=params(8 if resident else 24),
        cost_estimate=cost(2.5),
        name="backward_early",
    )(pinned(dense, resident), mine)


def backward_late(dense, early, siblings, columns, nodes, resident):
    wide, half = siblings.shape
    first = columns[0]

    def kernel(dense_ref, early_ref, siblings_ref, *out_refs):
        step = pl.program_id(0)
        for i, m in enumerate(columns):

            @pl.when(step == i)
            def _():
                if resident:
                    block = dense_ref[half : 2 * half, m * nodes : (m + 1) * nodes]
                else:
                    block = dense_ref[...]
                out = jnp.dot(siblings_ref[...], block, preferred_element_type=F32)
                out_refs[i][...] = (early_ref[0] + out).astype(out_refs[i].dtype)

    spec = vmem() if resident else pl.BlockSpec((half, nodes), lambda i: (1, i + first))
    whole = lambda shape: pl.BlockSpec(shape, lambda i: (0,) * len(shape))
    outs = [sds((wide, nodes), F32 if m == 0 else BF16) for m in columns]
    return pl.pallas_call(
        kernel,
        out_shape=outs,
        grid=(len(columns),),
        in_specs=[
            spec,
            pl.BlockSpec((1, wide, nodes), lambda i: (i + first, 0, 0)),
            whole((wide, half)),
        ],
        out_specs=[whole(o.shape) for o in outs],
        compiler_params=params(10 if resident else 32),
        cost_estimate=cost(1.5),
        name="backward_late",
    )(pinned(dense, resident), early, siblings)


def share_total(pieces):
    height, columns = pieces[0].shape
    share = height - BIAS_ROWS
    width = columns // 2

    def kernel(*refs):
        share_ref, bias_ref = refs[-2:]
        terms = [ref[...] for ref in refs[:-2]]
        while len(terms) > 1:
            terms = [terms[i] + terms[i + 1] for i in range(0, len(terms), 2)]
        share_ref[...] = terms[0][0:share]
        bias_ref[...] = terms[0][share : share + 1, 0:width]

    return pl.pallas_call(
        kernel,
        out_shape=[sds((share, columns), F32), sds((1, width), F32)],
        in_specs=[vmem()] * len(pieces),
        out_specs=[vmem()] * 2,
        compiler_params=params(8),
        cost_estimate=cost(0.1),
        name="share_total",
    )(*pieces)


def join(pieces):
    height, columns = pieces[0].shape

    def kernel(*refs):
        for j, ref in enumerate(refs[:-1]):
            refs[-1][j * height : (j + 1) * height, :] = ref[...]

    return pl.pallas_call(
        kernel,
        out_shape=sds((len(pieces) * height, columns), F32),
        in_specs=[vmem()] * len(pieces),
        out_specs=vmem(),
        compiler_params=params(4),
        cost_estimate=cost(0.1),
        name="join",
    )(*pieces)


def weight_grads(mine, siblings, n_row):
    chips = n_row // 2
    share = mine.shape[0] // chips
    width = mine.shape[1] // 2

    def kernel(mine_ref, siblings_ref, self_ref, neigh_ref):
        chip = lax.axis_index("row") // 2
        core = lax.axis_index("row") % 2
        for k, ref in enumerate((mine_ref, siblings_ref)):
            for j in range(chips):
                at = pl.multiple_of(((chip ^ j) * 2 + (core ^ k)) * share, share)
                low = j * share
                self_ref[pl.ds(at, share), :] = ref[low : low + share, 0:width]
                neigh_ref[pl.ds(at, share), :] = ref[low : low + share, width:]

    return pl.pallas_call(
        kernel,
        out_shape=[sds((width, width), F32)] * 2,
        in_specs=[vmem()] * 2,
        out_specs=[vmem()] * 2,
        compiler_params=params(8),
        cost_estimate=cost(1),
        name="weight_grads",
    )(mine, siblings)


def finish(d_pre, w_self, own, arrived):
    nodes, width = d_pre.shape

    def kernel(d_pre_ref, ws_ref, own_ref, *refs):
        out_ref = refs[-1]
        direct = lax.dot_general(
            d_pre_ref[...], ws_ref[...], (((1,), (1,)), ((), ())), preferred_element_type=F32
        )
        acc = own_ref[...]
        for ref in refs[:-1]:
            acc = acc + ref[...].astype(F32)
        out_ref[...] = (direct + jnp.transpose(acc)).astype(BF16)

    return pl.pallas_call(
        kernel,
        out_shape=sds((nodes, width), BF16),
        in_specs=[vmem()] * (3 + len(arrived)),
        out_specs=vmem(),
        compiler_params=params(8),
        cost_estimate=cost(1),
        name="finish",
    )(d_pre, w_self, own, *arrived)


def swap(x, axis, mask):
    size = lax.axis_size(axis)
    return lax.ppermute(x, axis, [(i, i ^ mask) for i in range(size)])


def far_first(n):
    return sorted(range(1, n), key=lambda m: -bin(m).count("1") * n - m)


def body(features, degree, cotangent, tile_values, tile_row, tile_col, w_self, w_neigh, bias):
    nodes, width = features.shape
    tile = tile_values.shape[1]
    n_row = lax.axis_size("row")
    n_col = lax.axis_size("col")
    chips = n_row // 2
    per_dev = nodes // tile
    resident = n_row * nodes * n_col * nodes * 2 <= RESIDENT_BYTES

    source = {m: swap(features, "col", m) for m in far_first(n_col)}
    source[0] = features
    build = densify if resident else densify_far
    dense = build(tile_values, tile_row, tile_col, n_row, n_col, per_dev)

    last = n_col // 2
    last_piece = source.pop(last)
    early = forward_early(dense, source, n_row, resident)

    def late(first, count, dtype):
        return forward_late(dense, early, last, last_piece, first, count, dtype, resident)

    give = late(chips + 1, chips - 1, BF16)
    got = swap(give, "row", 1)
    keep = late(1, chips - 1, F32)
    sends = add_parts(keep, got)
    arrivals = [swap(sends[j - 1], "row", 2 * j) for j in range(1, chips)]
    give_own = late(chips, 1, BF16)
    got_own = swap(give_own, "row", 1)
    keep_own = late(0, 1, F32)
    hidden, neigh_mean, d_pre, d_agg = middle(
        features,
        degree[None, :],
        cotangent,
        w_self,
        w_neigh,
        bias[None, :],
        keep_own,
        got_own,
        arrivals,
    )

    pieces = [d_agg] + [swap(d_agg, "row", 2 * j) for j in range(1, chips)]

    kept, sent = local_grads(features, neigh_mean, d_pre, n_row)
    total = add_sent(kept, swap(sent, "row", 1), BF16)
    mask = n_col // 2
    while mask > 1:
        total = add_sent(total, swap(total, "col", mask), BF16)
        mask //= 2
    pieces, total = lax.optimization_barrier((pieces, total))
    mine = side_by_side(pieces)
    siblings = swap(mine, "row", 1)
    got_last = swap(total, "col", 1)

    early = backward_early(dense, mine, n_col, nodes, resident)
    far_columns, near_columns = list(range(n_col // 2, n_col)), list(range(n_col // 2))
    far = backward_late(dense, early, siblings, far_columns, nodes, resident)
    own, *near = backward_late(dense, early, siblings, near_columns, nodes, resident)
    far_back = tuple(swap(x, "col", m) for m, x in zip(far_columns, far))
    near_back = [swap(x, "col", m) for m, x in zip(near_columns[1:], near)]

    got_last, _ = lax.optimization_barrier((got_last, far))
    cuts = chip_parts(add_sent(total, got_last, F32), n_row)
    arrivals = [swap(cuts[j], "row", 2 * j) for j in range(1, chips)]
    piece, grad_bias = share_total([cuts[0]] + arrivals)
    shares = join([piece] + [swap(piece, "row", 2 * j) for j in range(1, chips)])
    shares, far_back = lax.optimization_barrier((shares, far_back))
    grad_self, grad_neigh = weight_grads(shares, swap(shares, "row", 1), n_row)
    grad_x = finish(d_pre, w_self, own, [*near_back, *far_back])
    return (hidden, grad_x, grad_self, grad_neigh, grad_bias.reshape(width))


def solution(mesh):
    placed = (
        P(("col", "row"), None),
        P(("col", "row")),
        P(("col", "row"), None),
        P(("col", "row"), None, None),
        P(("col", "row")),
        P(("col", "row")),
        P(),
        P(),
        P(),
    )
    return jax.shard_map(
        body,
        mesh=mesh,
        in_specs=placed,
        out_specs=(P(("col", "row"), None), P(("col", "row"), None), P(), P(), P()),
        check_vma=False,
    )
```

```python
import jax
import jax.numpy as jnp
from jax import lax
from jax.experimental import pallas as pl
from jax.experimental.pallas import tpu as pltpu
from jax.sharding import PartitionSpec as P

F32 = jnp.float32
BF16 = jnp.bfloat16
MIB = 1 << 20
RESIDENT_BYTES = 20 * MIB
BIAS_ROWS = 16


def vmem():
    return pl.BlockSpec(memory_space=pltpu.VMEM)


def params(limit_mib):
    return pltpu.CompilerParams(vmem_limit_bytes=limit_mib * MIB)


def cost(us):
    return pl.CostEstimate(flops=0, bytes_accessed=int(us * 3.7e6), transcendentals=0)


def sds(shape, dtype):
    return jax.ShapeDtypeStruct(shape, dtype)


def densify_far(tile_values, tile_row, tile_col, n_row, n_col, per_dev):
    slots, tile, _ = tile_values.shape
    chips = n_row // 2
    rows = n_row * per_dev
    cols = n_col * per_dev
    cells = rows * cols

    def kernel(row_ref, col_ref, values_ref, dense_ref, table, blank, sem):
        blank[...] = jnp.zeros_like(blank)
        chip = lax.axis_index("row") // 2
        core = lax.axis_index("row") % 2
        col_at = lax.axis_index("col")

        def clear(i, carry):
            for k in range(8):
                table[i * 8 + k] = slots
            return carry

        lax.fori_loop(0, cells // 8, clear, 0)

        def note(i, carry):
            for k in range(4):
                at = i * 4 + k
                table[row_ref[at] * cols + col_ref[at]] = at
            return carry

        lax.fori_loop(0, slots // 4, note, 0)

        def fill(i, carry):
            slot = table[i]
            t = i // cols
            s = i % cols
            owner = t // per_dev
            block = ((owner % 2) ^ core) * chips + ((owner // 2) ^ chip)
            u = (block * per_dev + t % per_dev) * tile
            v = (((s // per_dev) ^ col_at) * per_dev + s % per_dev) * tile
            where = dense_ref.at[
                pl.ds(pl.multiple_of(u, tile), tile), pl.ds(pl.multiple_of(v, tile), tile)
            ]

            @pl.when(slot < slots)
            def _():
                pltpu.make_async_copy(values_ref.at[slot], where, sem).start()

            @pl.when(slot >= slots)
            def _():
                pltpu.make_async_copy(blank, where, sem).start()

            return carry

        lax.fori_loop(0, cells, fill, 0)
        pltpu.make_async_copy(dense_ref, dense_ref, sem).wait()

    shape = (rows * tile, cols * tile)
    return pl.pallas_call(
        kernel,
        out_shape=sds(shape, BF16),
        grid_spec=pltpu.PrefetchScalarGridSpec(
            num_scalar_prefetch=2,
            grid=(),
            in_specs=[pl.BlockSpec(memory_space=pl.ANY)],
            out_specs=pl.BlockSpec(memory_space=pl.ANY),
            scratch_shapes=[
                pltpu.SMEM((cells + cols,), jnp.int32),
                pltpu.VMEM((tile, tile), BF16),
                pltpu.SemaphoreType.DMA,
            ],
        ),
        compiler_params=params(8),
        cost_estimate=cost(40),
        name="densify_far",
    )(tile_row, tile_col, tile_values)


def densify(tile_values, tile_row, tile_col, n_row, n_col, per_dev):
    slots, tile, _ = tile_values.shape
    chips = n_row // 2
    rows = n_row * per_dev
    cols = n_col * per_dev
    chip = lax.axis_index("row") // 2
    core = lax.axis_index("row") % 2
    owner = tile_row // per_dev
    block = ((owner % 2) ^ core) * chips + ((owner // 2) ^ chip)
    down = (block * per_dev + tile_row % per_dev) * tile
    down = jnp.where(tile_row < rows, down, rows * tile)
    right = ((tile_col // per_dev) ^ lax.axis_index("col")) * per_dev + tile_col % per_dev
    right = right * tile
    step_slots = 32
    while slots % step_slots:
        step_slots //= 2

    def kernel(down_ref, right_ref, values_ref, dense_ref):
        step = pl.program_id(0)

        @pl.when(step == 0)
        def _():
            def clear(i, carry):
                at = pl.multiple_of(i * tile, tile)
                dense_ref[pl.ds(at, tile), :] = jnp.zeros((tile, cols * tile), BF16)
                return carry

            lax.fori_loop(0, rows, clear, 0)

        for k in range(step_slots):
            u = pl.multiple_of(down_ref[step * step_slots + k], tile)
            v = pl.multiple_of(right_ref[step * step_slots + k], tile)
            dense_ref[pl.ds(u, tile), pl.ds(v, tile)] = values_ref[k]

    return pl.pallas_call(
        kernel,
        out_shape=pltpu.VMEM(((rows + 1) * tile, cols * tile), BF16),
        grid_spec=pltpu.PrefetchScalarGridSpec(
            num_scalar_prefetch=2,
            grid=(slots // step_slots,),
            in_specs=[pl.BlockSpec((step_slots, tile, tile), lambda i, *_: (i, 0, 0))],
            out_specs=vmem(),
        ),
        compiler_params=params(8),
        cost_estimate=cost(10),
        name="densify",
    )(down, right, pltpu.with_memory_space_constraint(tile_values, pltpu.HBM))


def pinned(dense, resident):
    return pltpu.with_memory_space_constraint(dense, pltpu.VMEM) if resident else dense


def forward_early(dense, sources, n_row, resident):
    places = sorted(sources)
    nodes, width = sources[places[0]].shape
    cols = dense.shape[1]

    def kernel(dense_ref, *refs):
        out_ref = refs[-1]
        rows = pl.ds(pl.multiple_of(pl.program_id(0) * nodes, nodes), nodes) if resident else slice(None)
        total = None
        for m, ref in zip(places, refs[:-1]):
            block = dense_ref[rows, m * nodes : (m + 1) * nodes]
            out = jnp.dot(block, ref[...], preferred_element_type=F32)
            total = out if total is None else total + out
        out_ref[0] = total

    spec = vmem() if resident else pl.BlockSpec((nodes, cols), lambda i: (i, 0))
    return pl.pallas_call(
        kernel,
        out_shape=sds((n_row, nodes, width), F32),
        grid=(n_row,),
        in_specs=[spec] + [pl.BlockSpec((nodes, width), lambda i: (0, 0))] * len(places),
        out_specs=pl.BlockSpec((1, nodes, width), lambda i: (i, 0, 0)),
        compiler_params=params(8 if resident else 32),
        cost_estimate=cost(5),
        name="forward_early",
    )(pinned(dense, resident), *[sources[m] for m in places])


def forward_late(dense, early, place, piece, first, count, dtype, resident):
    nodes, width = piece.shape

    def kernel(dense_ref, early_ref, piece_ref, out_ref):
        if resident:
            at = pl.multiple_of((first + pl.program_id(0)) * nodes, nodes)
            block = dense_ref[pl.ds(at, nodes), place * nodes : (place + 1) * nodes]
        else:
            block = dense_ref[...]
        out = jnp.dot(block, piece_ref[...], preferred_element_type=F32)
        out_ref[0] = (early_ref[0] + out).astype(dtype)

    spec = vmem() if resident else pl.BlockSpec((nodes, nodes), lambda i: (i + first, place))
    return pl.pallas_call(
        kernel,
        out_shape=sds((count, nodes, width), dtype),
        grid=(count,),
        in_specs=[
            spec,
            pl.BlockSpec((1, nodes, width), lambda i: (i + first, 0, 0)),
            pl.BlockSpec((nodes, width), lambda i: (0, 0)),
        ],
        out_specs=pl.BlockSpec((1, nodes, width), lambda i: (i, 0, 0)),
        compiler_params=params(8),
        cost_estimate=cost(1),
        name="forward_late",
    )(pinned(dense, resident), early, piece)


def add_parts(keep, got):
    count, nodes, wide = keep.shape

    def kernel(keep_ref, got_ref, *out_refs):
        for j in range(count):
            out_refs[j][...] = (keep_ref[j] + got_ref[j].astype(F32)).astype(BF16)

    return pl.pallas_call(
        kernel,
        out_shape=[sds((nodes, wide), BF16)] * count,
        in_specs=[vmem()] * 2,
        out_specs=[vmem()] * count,
        compiler_params=params(8),
        cost_estimate=cost(0.1),
        name="add_parts",
    )(keep, got)


def middle(features, degree, cotangent, w_self, w_neigh, bias, keep, got, arrivals):
    nodes, width = features.shape

    def kernel(*refs):
        feat_ref, degree_ref, cot_ref, ws_ref, wn_ref, bias_ref = refs[:6]
        keep_ref, got_ref, *part_refs = refs[6:-4]
        hidden_ref, mean_ref, d_pre_ref, d_agg_ref = refs[-4:]
        scale = degree_ref[...].astype(F32)
        scale_down = jnp.transpose(jnp.broadcast_to(scale, (width, nodes)))
        total = keep_ref[0] + got_ref[0].astype(F32)
        for ref in part_refs:
            total = total + ref[...].astype(F32)
        neigh_mean = (total / scale_down).astype(BF16)
        mean_ref[...] = neigh_mean
        pre = jnp.dot(feat_ref[...], ws_ref[...], preferred_element_type=F32)
        pre = pre + jnp.dot(neigh_mean, wn_ref[...], preferred_element_type=F32) + bias_ref[...]
        sig = jax.nn.sigmoid(pre)
        hidden_ref[...] = (pre * sig).astype(BF16)
        d_pre = (cot_ref[...].astype(F32) * sig * (1.0 + pre * (1.0 - sig))).astype(BF16)
        d_pre_ref[...] = d_pre
        d_agg = lax.dot_general(
            d_pre, wn_ref[...], (((1,), (1,)), ((), ())), preferred_element_type=F32
        )
        d_agg_ref[...] = (jnp.transpose(d_agg) / scale).astype(BF16)

    args = [features, degree, cotangent, w_self, w_neigh, bias, keep, got, *arrivals]
    return pl.pallas_call(
        kernel,
        out_shape=[sds((nodes, width), BF16)] * 3 + [sds((width, nodes), BF16)],
        in_specs=[vmem()] * len(args),
        out_specs=[vmem()] * 4,
        compiler_params=params(12),
        cost_estimate=cost(1.5),
        name="middle",
    )(*args)


def local_grads(features, neigh_mean, d_pre, n_row):
    nodes, width = features.shape
    share = width // n_row
    half = width // 2

    def kernel(feat_ref, mean_ref, d_pre_ref, keep_ref, give_ref, grads_ref):
        d_pre_now = d_pre_ref[...]
        over = (((0,), (0,)), ((), ()))
        grads_ref[:, 0:width] = lax.dot_general(
            feat_ref[...], d_pre_now, over, preferred_element_type=F32
        )
        grads_ref[:, width:] = lax.dot_general(
            mean_ref[...], d_pre_now, over, preferred_element_type=F32
        )
        bias_sum = jnp.sum(d_pre_now.astype(F32), axis=0, keepdims=True)
        bias_row = jnp.concatenate([bias_sum, bias_sum], axis=1)
        bias_rows = jnp.broadcast_to(bias_row, (BIAS_ROWS, 2 * width))
        core = lax.axis_index("row") % 2
        for k, ref in enumerate((keep_ref, give_ref)):
            for j in range(n_row // 2):
                at = pl.multiple_of((j * 2 + (core ^ k)) * share, share)
                ref[j * share : (j + 1) * share, :] = grads_ref[pl.ds(at, share), :].astype(ref.dtype)
            ref[half:, :] = bias_rows.astype(BF16).astype(ref.dtype)

    return pl.pallas_call(
        kernel,
        out_shape=[sds((half + BIAS_ROWS, 2 * width), d) for d in (F32, BF16)],
        in_specs=[vmem()] * 3,
        out_specs=[vmem()] * 2,
        scratch_shapes=[pltpu.VMEM((width, 2 * width), F32)],
        compiler_params=params(8),
        cost_estimate=cost(0.5),
        name="local_grads",
    )(features, neigh_mean, d_pre)


def add_sent(keep, got, kind):
    def kernel(keep_ref, got_ref, out_ref):
        out_ref[...] = (keep_ref[...].astype(F32) + got_ref[...].astype(F32)).astype(kind)

    return pl.pallas_call(
        kernel,
        out_shape=sds(keep.shape, kind),
        in_specs=[vmem()] * 2,
        out_specs=vmem(),
        compiler_params=params(8),
        cost_estimate=cost(0.1),
        name="add_sent",
    )(keep, got)


def chip_parts(half, n_row):
    height, columns = half.shape
    rows = height - BIAS_ROWS
    chips = n_row // 2
    share = rows // chips

    def kernel(half_ref, *out_refs):
        chip = lax.axis_index("row") // 2
        for j, ref in enumerate(out_refs):
            at = pl.multiple_of((chip ^ j) * share, share)
            ref[0:share, :] = half_ref[pl.ds(at, share), :]
            ref[share:, :] = half_ref[rows:, :]

    return pl.pallas_call(
        kernel,
        out_shape=[sds((share + BIAS_ROWS, columns), F32)] * chips,
        in_specs=[vmem()],
        out_specs=[vmem()] * chips,
        compiler_params=params(8),
        cost_estimate=cost(0.1),
        name="chip_parts",
    )(half)


def side_by_side(pieces):
    wide, nodes = pieces[0].shape

    def kernel(*refs):
        for j, ref in enumerate(refs[:-1]):
            refs[-1][:, j * nodes : (j + 1) * nodes] = ref[...]

    return pl.pallas_call(
        kernel,
        out_shape=sds((wide, len(pieces) * nodes), BF16),
        in_specs=[vmem()] * len(pieces),
        out_specs=vmem(),
        compiler_params=params(8),
        cost_estimate=cost(0.3),
        name="side_by_side",
    )(*pieces)


def backward_early(dense, mine, n_col, nodes, resident):
    wide, half = mine.shape

    def kernel(dense_ref, mine_ref, out_ref):
        if resident:
            at = pl.multiple_of(pl.program_id(0) * nodes, nodes)
            block = dense_ref[0:half, pl.ds(at, nodes)]
        else:
            block = dense_ref[...]
        out_ref[0] = jnp.dot(mine_ref[...], block, preferred_element_type=F32)

    spec = vmem() if resident else pl.BlockSpec((half, nodes), lambda i: (0, i))
    return pl.pallas_call(
        kernel,
        out_shape=sds((n_col, wide, nodes), F32),
        grid=(n_col,),
        in_specs=[spec, pl.BlockSpec((wide, half), lambda i: (0, 0))],
        out_specs=pl.BlockSpec((1, wide, nodes), lambda i: (i, 0, 0)),
        compiler_params=params(8 if resident else 24),
        cost_estimate=cost(2.5),
        name="backward_early",
    )(pinned(dense, resident), mine)


def backward_late(dense, early, siblings, columns, nodes, resident):
    wide, half = siblings.shape
    first = columns[0]

    def kernel(dense_ref, early_ref, siblings_ref, *out_refs):
        step = pl.program_id(0)
        for i, m in enumerate(columns):

            @pl.when(step == i)
            def _():
                if resident:
                    block = dense_ref[half : 2 * half, m * nodes : (m + 1) * nodes]
                else:
                    block = dense_ref[...]
                out = jnp.dot(siblings_ref[...], block, preferred_element_type=F32)
                out_refs[i][...] = (early_ref[0] + out).astype(out_refs[i].dtype)

    spec = vmem() if resident else pl.BlockSpec((half, nodes), lambda i: (1, i + first))
    whole = lambda shape: pl.BlockSpec(shape, lambda i: (0,) * len(shape))
    outs = [sds((wide, nodes), F32 if m == 0 else BF16) for m in columns]
    return pl.pallas_call(
        kernel,
        out_shape=outs,
        grid=(len(columns),),
        in_specs=[
            spec,
            pl.BlockSpec((1, wide, nodes), lambda i: (i + first, 0, 0)),
            whole((wide, half)),
        ],
        out_specs=[whole(o.shape) for o in outs],
        compiler_params=params(10 if resident else 32),
        cost_estimate=cost(1.5),
        name="backward_late",
    )(pinned(dense, resident), early, siblings)


def share_total(pieces):
    height, columns = pieces[0].shape
    share = height - BIAS_ROWS
    width = columns // 2

    def kernel(*refs):
        share_ref, bias_ref = refs[-2:]
        terms = [ref[...] for ref in refs[:-2]]
        while len(terms) > 1:
            terms = [terms[i] + terms[i + 1] for i in range(0, len(terms), 2)]
        share_ref[...] = terms[0][0:share]
        bias_ref[...] = terms[0][share : share + 1, 0:width]

    return pl.pallas_call(
        kernel,
        out_shape=[sds((share, columns), F32), sds((1, width), F32)],
        in_specs=[vmem()] * len(pieces),
        out_specs=[vmem()] * 2,
        compiler_params=params(8),
        cost_estimate=cost(0.1),
        name="share_total",
    )(*pieces)


def join(pieces):
    height, columns = pieces[0].shape

    def kernel(*refs):
        for j, ref in enumerate(refs[:-1]):
            refs[-1][j * height : (j + 1) * height, :] = ref[...]

    return pl.pallas_call(
        kernel,
        out_shape=sds((len(pieces) * height, columns), F32),
        in_specs=[vmem()] * len(pieces),
        out_specs=vmem(),
        compiler_params=params(4),
        cost_estimate=cost(0.1),
        name="join",
    )(*pieces)


def finish(mine, siblings, d_pre, w_self, own, arrived, n_row):
    chips = n_row // 2
    share = mine.shape[0] // chips
    nodes, width = d_pre.shape

    def kernel(mine_ref, siblings_ref, d_pre_ref, ws_ref, own_ref, *refs):
        self_ref, neigh_ref, out_ref = refs[-3:]
        chip = lax.axis_index("row") // 2
        core = lax.axis_index("row") % 2
        for k, ref in enumerate((mine_ref, siblings_ref)):
            for j in range(chips):
                at = pl.multiple_of(((chip ^ j) * 2 + (core ^ k)) * share, share)
                low = j * share
                self_ref[pl.ds(at, share), :] = ref[low : low + share, 0:width]
                neigh_ref[pl.ds(at, share), :] = ref[low : low + share, width:]
        direct = lax.dot_general(
            d_pre_ref[...], ws_ref[...], (((1,), (1,)), ((), ())), preferred_element_type=F32
        )
        acc = own_ref[...]
        for ref in refs[:-3]:
            acc = acc + ref[...].astype(F32)
        out_ref[...] = (direct + jnp.transpose(acc)).astype(BF16)

    return pl.pallas_call(
        kernel,
        out_shape=[sds((width, width), F32)] * 2 + [sds((nodes, width), BF16)],
        in_specs=[vmem()] * (5 + len(arrived)),
        out_specs=[vmem()] * 3,
        compiler_params=params(12),
        cost_estimate=cost(1),
        name="finish",
    )(mine, siblings, d_pre, w_self, own, *arrived)


def swap(x, axis, mask):
    size = lax.axis_size(axis)
    return lax.ppermute(x, axis, [(i, i ^ mask) for i in range(size)])


def far_first(n):
    return sorted(range(1, n), key=lambda m: -bin(m).count("1") * n - m)


def body(features, degree, cotangent, tile_values, tile_row, tile_col, w_self, w_neigh, bias):
    nodes, width = features.shape
    tile = tile_values.shape[1]
    n_row = lax.axis_size("row")
    n_col = lax.axis_size("col")
    chips = n_row // 2
    per_dev = nodes // tile
    resident = n_row * nodes * n_col * nodes * 2 <= RESIDENT_BYTES

    source = {m: swap(features, "col", m) for m in far_first(n_col)}
    source[0] = features
    build = densify if resident else densify_far
    dense = build(tile_values, tile_row, tile_col, n_row, n_col, per_dev)

    last = n_col // 2
    last_piece = source.pop(last)
    early = forward_early(dense, source, n_row, resident)

    def late(first, count, dtype):
        return forward_late(dense, early, last, last_piece, first, count, dtype, resident)

    give = late(chips + 1, chips - 1, BF16)
    got = swap(give, "row", 1)
    keep = late(1, chips - 1, F32)
    sends = add_parts(keep, got)
    arrivals = [swap(sends[j - 1], "row", 2 * j) for j in range(1, chips)]
    give_own = late(chips, 1, BF16)
    got_own = swap(give_own, "row", 1)
    keep_own = late(0, 1, F32)
    hidden, neigh_mean, d_pre, d_agg = middle(
        features,
        degree[None, :],
        cotangent,
        w_self,
        w_neigh,
        bias[None, :],
        keep_own,
        got_own,
        arrivals,
    )

    pieces = [d_agg] + [swap(d_agg, "row", 2 * j) for j in range(1, chips)]

    kept, sent = local_grads(features, neigh_mean, d_pre, n_row)
    total = add_sent(kept, swap(sent, "row", 1), BF16)
    mask = n_col // 2
    while mask > 1:
        total = add_sent(total, swap(total, "col", mask), BF16)
        mask //= 2
    pieces, total = lax.optimization_barrier((pieces, total))
    mine = side_by_side(pieces)
    siblings = swap(mine, "row", 1)
    got_last = swap(total, "col", 1)

    early = backward_early(dense, mine, n_col, nodes, resident)
    far_columns, near_columns = list(range(n_col // 2, n_col)), list(range(n_col // 2))
    far = backward_late(dense, early, siblings, far_columns, nodes, resident)
    own, *near = backward_late(dense, early, siblings, near_columns, nodes, resident)
    far_back = tuple(swap(x, "col", m) for m, x in zip(far_columns, far))
    near_back = [swap(x, "col", m) for m, x in zip(near_columns[1:], near)]

    got_last, _ = lax.optimization_barrier((got_last, far))
    cuts = chip_parts(add_sent(total, got_last, F32), n_row)
    arrivals = [swap(cuts[j], "row", 2 * j) for j in range(1, chips)]
    piece, grad_bias = share_total([cuts[0]] + arrivals)
    shares = join([piece] + [swap(piece, "row", 2 * j) for j in range(1, chips)])
    shares, far_back = lax.optimization_barrier((shares, far_back))
    siblings = swap(shares, "row", 1)
    back = [*near_back, *far_back]
    grad_self, grad_neigh, grad_x = finish(shares, siblings, d_pre, w_self, own, back, n_row)
    return (hidden, grad_x, grad_self, grad_neigh, grad_bias.reshape(width))


def solution(mesh):
    placed = (
        P(("col", "row"), None),
        P(("col", "row")),
        P(("col", "row"), None),
        P(("col", "row"), None, None),
        P(("col", "row")),
        P(("col", "row")),
        P(),
        P(),
        P(),
    )
    return jax.shard_map(
        body,
        mesh=mesh,
        in_specs=placed,
        out_specs=(P(("col", "row"), None), P(("col", "row"), None), P(), P(), P()),
        check_vma=False,
    )
```

```python
import jax
import jax.numpy as jnp
from jax import lax
from jax.experimental import pallas as pl
from jax.experimental.pallas import tpu as pltpu
from jax.sharding import PartitionSpec as P

F32 = jnp.float32
BF16 = jnp.bfloat16
MIB = 1 << 20
RESIDENT_BYTES = 20 * MIB
BIAS_ROWS = 16


def vmem():
    return pl.BlockSpec(memory_space=pltpu.VMEM)


def params(limit_mib):
    return pltpu.CompilerParams(vmem_limit_bytes=limit_mib * MIB)


def cost(us):
    return pl.CostEstimate(flops=0, bytes_accessed=int(us * 3.7e6), transcendentals=0)


def sds(shape, dtype):
    return jax.ShapeDtypeStruct(shape, dtype)


def densify_far(tile_values, tile_row, tile_col, n_row, n_col, per_dev):
    slots, tile, _ = tile_values.shape
    chips = n_row // 2
    rows = n_row * per_dev
    cols = n_col * per_dev
    cells = rows * cols

    def kernel(row_ref, col_ref, values_ref, dense_ref, table, blank, sem):
        blank[...] = jnp.zeros_like(blank)
        chip = lax.axis_index("row") // 2
        core = lax.axis_index("row") % 2
        col_at = lax.axis_index("col")

        def clear(i, carry):
            for k in range(8):
                table[i * 8 + k] = slots
            return carry

        lax.fori_loop(0, cells // 8, clear, 0)

        def note(i, carry):
            for k in range(4):
                at = i * 4 + k
                table[row_ref[at] * cols + col_ref[at]] = at
            return carry

        lax.fori_loop(0, slots // 4, note, 0)

        def fill(i, carry):
            slot = table[i]
            t = i // cols
            s = i % cols
            owner = t // per_dev
            block = ((owner % 2) ^ core) * chips + ((owner // 2) ^ chip)
            u = (block * per_dev + t % per_dev) * tile
            v = (((s // per_dev) ^ col_at) * per_dev + s % per_dev) * tile
            where = dense_ref.at[
                pl.ds(pl.multiple_of(u, tile), tile), pl.ds(pl.multiple_of(v, tile), tile)
            ]

            @pl.when(slot < slots)
            def _():
                pltpu.make_async_copy(values_ref.at[slot], where, sem).start()

            @pl.when(slot >= slots)
            def _():
                pltpu.make_async_copy(blank, where, sem).start()

            return carry

        lax.fori_loop(0, cells, fill, 0)
        pltpu.make_async_copy(dense_ref, dense_ref, sem).wait()

    shape = (rows * tile, cols * tile)
    return pl.pallas_call(
        kernel,
        out_shape=sds(shape, BF16),
        grid_spec=pltpu.PrefetchScalarGridSpec(
            num_scalar_prefetch=2,
            grid=(),
            in_specs=[pl.BlockSpec(memory_space=pl.ANY)],
            out_specs=pl.BlockSpec(memory_space=pl.ANY),
            scratch_shapes=[
                pltpu.SMEM((cells + cols,), jnp.int32),
                pltpu.VMEM((tile, tile), BF16),
                pltpu.SemaphoreType.DMA,
            ],
        ),
        compiler_params=params(8),
        cost_estimate=cost(40),
        name="densify_far",
    )(tile_row, tile_col, tile_values)


def densify(tile_values, tile_row, tile_col, n_row, n_col, per_dev):
    slots, tile, _ = tile_values.shape
    chips = n_row // 2
    rows = n_row * per_dev
    cols = n_col * per_dev
    chip = lax.axis_index("row") // 2
    core = lax.axis_index("row") % 2
    owner = tile_row // per_dev
    block = ((owner % 2) ^ core) * chips + ((owner // 2) ^ chip)
    down = (block * per_dev + tile_row % per_dev) * tile
    down = jnp.where(tile_row < rows, down, rows * tile)
    right = ((tile_col // per_dev) ^ lax.axis_index("col")) * per_dev + tile_col % per_dev
    right = right * tile
    step_slots = 32
    while slots % step_slots:
        step_slots //= 2

    def kernel(down_ref, right_ref, values_ref, dense_ref):
        step = pl.program_id(0)

        @pl.when(step == 0)
        def _():
            def clear(i, carry):
                at = pl.multiple_of(i * tile, tile)
                dense_ref[pl.ds(at, tile), :] = jnp.zeros((tile, cols * tile), BF16)
                return carry

            lax.fori_loop(0, rows, clear, 0)

        for k in range(step_slots):
            u = pl.multiple_of(down_ref[step * step_slots + k], tile)
            v = pl.multiple_of(right_ref[step * step_slots + k], tile)
            dense_ref[pl.ds(u, tile), pl.ds(v, tile)] = values_ref[k]

    return pl.pallas_call(
        kernel,
        out_shape=pltpu.VMEM(((rows + 1) * tile, cols * tile), BF16),
        grid_spec=pltpu.PrefetchScalarGridSpec(
            num_scalar_prefetch=2,
            grid=(slots // step_slots,),
            in_specs=[pl.BlockSpec((step_slots, tile, tile), lambda i, *_: (i, 0, 0))],
            out_specs=vmem(),
        ),
        compiler_params=params(8),
        cost_estimate=cost(10),
        name="densify",
    )(down, right, pltpu.with_memory_space_constraint(tile_values, pltpu.HBM))


def pinned(dense, resident):
    return pltpu.with_memory_space_constraint(dense, pltpu.VMEM) if resident else dense


def forward_early(dense, sources, n_row, resident):
    places = sorted(sources)
    nodes, width = sources[places[0]].shape
    cols = dense.shape[1]

    def kernel(dense_ref, *refs):
        out_ref = refs[-1]
        rows = pl.ds(pl.multiple_of(pl.program_id(0) * nodes, nodes), nodes) if resident else slice(None)
        total = None
        for m, ref in zip(places, refs[:-1]):
            block = dense_ref[rows, m * nodes : (m + 1) * nodes]
            out = jnp.dot(block, ref[...], preferred_element_type=F32)
            total = out if total is None else total + out
        out_ref[0] = total

    spec = vmem() if resident else pl.BlockSpec((nodes, cols), lambda i: (i, 0))
    return pl.pallas_call(
        kernel,
        out_shape=sds((n_row, nodes, width), F32),
        grid=(n_row,),
        in_specs=[spec] + [pl.BlockSpec((nodes, width), lambda i: (0, 0))] * len(places),
        out_specs=pl.BlockSpec((1, nodes, width), lambda i: (i, 0, 0)),
        compiler_params=params(8 if resident else 32),
        cost_estimate=cost(5),
        name="forward_early",
    )(pinned(dense, resident), *[sources[m] for m in places])


def forward_late(dense, early, place, piece, first, count, dtype, resident):
    nodes, width = piece.shape

    def kernel(dense_ref, early_ref, piece_ref, out_ref):
        if resident:
            at = pl.multiple_of((first + pl.program_id(0)) * nodes, nodes)
            block = dense_ref[pl.ds(at, nodes), place * nodes : (place + 1) * nodes]
        else:
            block = dense_ref[...]
        out = jnp.dot(block, piece_ref[...], preferred_element_type=F32)
        out_ref[0] = (early_ref[0] + out).astype(dtype)

    spec = vmem() if resident else pl.BlockSpec((nodes, nodes), lambda i: (i + first, place))
    return pl.pallas_call(
        kernel,
        out_shape=sds((count, nodes, width), dtype),
        grid=(count,),
        in_specs=[
            spec,
            pl.BlockSpec((1, nodes, width), lambda i: (i + first, 0, 0)),
            pl.BlockSpec((nodes, width), lambda i: (0, 0)),
        ],
        out_specs=pl.BlockSpec((1, nodes, width), lambda i: (i, 0, 0)),
        compiler_params=params(8),
        cost_estimate=cost(1),
        name="forward_late",
    )(pinned(dense, resident), early, piece)


def add_parts(keep, got):
    count, nodes, wide = keep.shape

    def kernel(keep_ref, got_ref, *out_refs):
        for j in range(count):
            out_refs[j][...] = (keep_ref[j] + got_ref[j].astype(F32)).astype(BF16)

    return pl.pallas_call(
        kernel,
        out_shape=[sds((nodes, wide), BF16)] * count,
        in_specs=[vmem()] * 2,
        out_specs=[vmem()] * count,
        compiler_params=params(8),
        cost_estimate=cost(0.1),
        name="add_parts",
    )(keep, got)


def middle(features, degree, cotangent, w_self, w_neigh, bias, keep, got, arrivals):
    nodes, width = features.shape

    def kernel(*refs):
        feat_ref, degree_ref, cot_ref, ws_ref, wn_ref, bias_ref = refs[:6]
        keep_ref, got_ref, *part_refs = refs[6:-4]
        hidden_ref, mean_ref, d_pre_ref, d_agg_ref = refs[-4:]
        scale = degree_ref[...].astype(F32)
        scale_down = jnp.transpose(jnp.broadcast_to(scale, (width, nodes)))
        total = keep_ref[0] + got_ref[0].astype(F32)
        for ref in part_refs:
            total = total + ref[...].astype(F32)
        neigh_mean = (total / scale_down).astype(BF16)
        mean_ref[...] = neigh_mean
        pre = jnp.dot(feat_ref[...], ws_ref[...], preferred_element_type=F32)
        pre = pre + jnp.dot(neigh_mean, wn_ref[...], preferred_element_type=F32) + bias_ref[...]
        sig = jax.nn.sigmoid(pre)
        hidden_ref[...] = (pre * sig).astype(BF16)
        d_pre = (cot_ref[...].astype(F32) * sig * (1.0 + pre * (1.0 - sig))).astype(BF16)
        d_pre_ref[...] = d_pre
        d_agg = lax.dot_general(
            d_pre, wn_ref[...], (((1,), (1,)), ((), ())), preferred_element_type=F32
        )
        d_agg_ref[...] = (jnp.transpose(d_agg) / scale).astype(BF16)

    args = [features, degree, cotangent, w_self, w_neigh, bias, keep, got, *arrivals]
    return pl.pallas_call(
        kernel,
        out_shape=[sds((nodes, width), BF16)] * 3 + [sds((width, nodes), BF16)],
        in_specs=[vmem()] * len(args),
        out_specs=[vmem()] * 4,
        compiler_params=params(12),
        cost_estimate=cost(1.5),
        name="middle",
    )(*args)


def local_grads(features, neigh_mean, d_pre, n_row):
    nodes, width = features.shape
    share = width // n_row
    half = width // 2

    def kernel(feat_ref, mean_ref, d_pre_ref, keep_ref, give_ref, grads_ref):
        d_pre_now = d_pre_ref[...]
        over = (((0,), (0,)), ((), ()))
        grads_ref[:, 0:width] = lax.dot_general(
            feat_ref[...], d_pre_now, over, preferred_element_type=F32
        )
        grads_ref[:, width:] = lax.dot_general(
            mean_ref[...], d_pre_now, over, preferred_element_type=F32
        )
        bias_sum = jnp.sum(d_pre_now.astype(F32), axis=0, keepdims=True)
        bias_row = jnp.concatenate([bias_sum, bias_sum], axis=1)
        bias_rows = jnp.broadcast_to(bias_row, (BIAS_ROWS, 2 * width))
        core = lax.axis_index("row") % 2
        for k, ref in enumerate((keep_ref, give_ref)):
            for j in range(n_row // 2):
                at = pl.multiple_of((j * 2 + (core ^ k)) * share, share)
                ref[j * share : (j + 1) * share, :] = grads_ref[pl.ds(at, share), :].astype(ref.dtype)
            ref[half:, :] = bias_rows.astype(BF16).astype(ref.dtype)

    return pl.pallas_call(
        kernel,
        out_shape=[sds((half + BIAS_ROWS, 2 * width), d) for d in (F32, BF16)],
        in_specs=[vmem()] * 3,
        out_specs=[vmem()] * 2,
        scratch_shapes=[pltpu.VMEM((width, 2 * width), F32)],
        compiler_params=params(8),
        cost_estimate=cost(0.5),
        name="local_grads",
    )(features, neigh_mean, d_pre)


def add_sent(keep, got, kind):
    def kernel(keep_ref, got_ref, out_ref):
        out_ref[...] = (keep_ref[...].astype(F32) + got_ref[...].astype(F32)).astype(kind)

    return pl.pallas_call(
        kernel,
        out_shape=sds(keep.shape, kind),
        in_specs=[vmem()] * 2,
        out_specs=vmem(),
        compiler_params=params(8),
        cost_estimate=cost(0.1),
        name="add_sent",
    )(keep, got)


def chip_parts(half, n_row):
    height, columns = half.shape
    rows = height - BIAS_ROWS
    chips = n_row // 2
    share = rows // chips

    def kernel(half_ref, *out_refs):
        chip = lax.axis_index("row") // 2
        for j, ref in enumerate(out_refs):
            at = pl.multiple_of((chip ^ j) * share, share)
            ref[0:share, :] = half_ref[pl.ds(at, share), :]
            ref[share:, :] = half_ref[rows:, :]

    return pl.pallas_call(
        kernel,
        out_shape=[sds((share + BIAS_ROWS, columns), F32)] * chips,
        in_specs=[vmem()],
        out_specs=[vmem()] * chips,
        compiler_params=params(8),
        cost_estimate=cost(0.1),
        name="chip_parts",
    )(half)


def side_by_side(pieces):
    wide, nodes = pieces[0].shape

    def kernel(*refs):
        for j, ref in enumerate(refs[:-1]):
            refs[-1][:, j * nodes : (j + 1) * nodes] = ref[...]

    return pl.pallas_call(
        kernel,
        out_shape=sds((wide, len(pieces) * nodes), BF16),
        in_specs=[vmem()] * len(pieces),
        out_specs=vmem(),
        compiler_params=params(8),
        cost_estimate=cost(0.3),
        name="side_by_side",
    )(*pieces)


def backward_early(dense, mine, n_col, nodes, resident):
    wide, half = mine.shape

    def kernel(dense_ref, mine_ref, out_ref):
        if resident:
            at = pl.multiple_of(pl.program_id(0) * nodes, nodes)
            block = dense_ref[0:half, pl.ds(at, nodes)]
        else:
            block = dense_ref[...]
        out_ref[0] = jnp.dot(mine_ref[...], block, preferred_element_type=F32)

    spec = vmem() if resident else pl.BlockSpec((half, nodes), lambda i: (0, i))
    return pl.pallas_call(
        kernel,
        out_shape=sds((n_col, wide, nodes), F32),
        grid=(n_col,),
        in_specs=[spec, pl.BlockSpec((wide, half), lambda i: (0, 0))],
        out_specs=pl.BlockSpec((1, wide, nodes), lambda i: (i, 0, 0)),
        compiler_params=params(8 if resident else 24),
        cost_estimate=cost(2.5),
        name="backward_early",
    )(pinned(dense, resident), mine)


def backward_late(dense, early, siblings, columns, nodes, resident):
    wide, half = siblings.shape
    first = columns[0]

    def kernel(dense_ref, early_ref, siblings_ref, *out_refs):
        step = pl.program_id(0)
        for i, m in enumerate(columns):

            @pl.when(step == i)
            def _():
                if resident:
                    block = dense_ref[half : 2 * half, m * nodes : (m + 1) * nodes]
                else:
                    block = dense_ref[...]
                out = jnp.dot(siblings_ref[...], block, preferred_element_type=F32)
                out_refs[i][...] = (early_ref[0] + out).astype(out_refs[i].dtype)

    spec = vmem() if resident else pl.BlockSpec((half, nodes), lambda i: (1, i + first))
    whole = lambda shape: pl.BlockSpec(shape, lambda i: (0,) * len(shape))
    outs = [sds((wide, nodes), F32 if m == 0 else BF16) for m in columns]
    return pl.pallas_call(
        kernel,
        out_shape=outs,
        grid=(len(columns),),
        in_specs=[
            spec,
            pl.BlockSpec((1, wide, nodes), lambda i: (i + first, 0, 0)),
            whole((wide, half)),
        ],
        out_specs=[whole(o.shape) for o in outs],
        compiler_params=params(10 if resident else 32),
        cost_estimate=cost(1.5),
        name="backward_late",
    )(pinned(dense, resident), early, siblings)


def share_total(pieces):
    height, columns = pieces[0].shape
    share = height - BIAS_ROWS
    width = columns // 2

    def kernel(*refs):
        share_ref, bias_ref = refs[-2:]
        terms = [ref[...] for ref in refs[:-2]]
        while len(terms) > 1:
            terms = [terms[i] + terms[i + 1] for i in range(0, len(terms), 2)]
        share_ref[...] = terms[0][0:share]
        bias_ref[...] = terms[0][share : share + 1, 0:width]

    return pl.pallas_call(
        kernel,
        out_shape=[sds((share, columns), F32), sds((1, width), F32)],
        in_specs=[vmem()] * len(pieces),
        out_specs=[vmem()] * 2,
        compiler_params=params(8),
        cost_estimate=cost(0.1),
        name="share_total",
    )(*pieces)


def join(pieces):
    height, columns = pieces[0].shape

    def kernel(*refs):
        for j, ref in enumerate(refs[:-1]):
            refs[-1][j * height : (j + 1) * height, :] = ref[...]

    return pl.pallas_call(
        kernel,
        out_shape=sds((len(pieces) * height, columns), F32),
        in_specs=[vmem()] * len(pieces),
        out_specs=vmem(),
        compiler_params=params(4),
        cost_estimate=cost(0.1),
        name="join",
    )(*pieces)


def finish(mine, siblings, d_pre, w_self, own, arrived, n_row):
    chips = n_row // 2
    share = mine.shape[0] // chips
    nodes, width = d_pre.shape

    def kernel(mine_ref, siblings_ref, d_pre_ref, ws_ref, own_ref, *refs):
        self_ref, neigh_ref, out_ref = refs[-3:]
        chip = lax.axis_index("row") // 2
        core = lax.axis_index("row") % 2
        for k, ref in enumerate((mine_ref, siblings_ref)):
            for j in range(chips):
                at = pl.multiple_of(((chip ^ j) * 2 + (core ^ k)) * share, share)
                low = j * share
                self_ref[pl.ds(at, share), :] = ref[low : low + share, 0:width]
                neigh_ref[pl.ds(at, share), :] = ref[low : low + share, width:]
        direct = lax.dot_general(
            d_pre_ref[...], ws_ref[...], (((1,), (1,)), ((), ())), preferred_element_type=F32
        )
        acc = own_ref[...]
        for ref in refs[:-3]:
            acc = acc + ref[...].astype(F32)
        out_ref[...] = (direct + jnp.transpose(acc)).astype(BF16)

    return pl.pallas_call(
        kernel,
        out_shape=[sds((width, width), F32)] * 2 + [sds((nodes, width), BF16)],
        in_specs=[vmem()] * (5 + len(arrived)),
        out_specs=[vmem()] * 3,
        compiler_params=params(12),
        cost_estimate=cost(1),
        name="finish",
    )(mine, siblings, d_pre, w_self, own, *arrived)


def swap(x, axis, mask):
    size = lax.axis_size(axis)
    return lax.ppermute(x, axis, [(i, i ^ mask) for i in range(size)])


def far_first(n):
    return sorted(range(1, n), key=lambda m: -bin(m).count("1") * n - m)


def body(features, degree, cotangent, tile_values, tile_row, tile_col, w_self, w_neigh, bias):
    nodes, width = features.shape
    tile = tile_values.shape[1]
    n_row = lax.axis_size("row")
    n_col = lax.axis_size("col")
    chips = n_row // 2
    per_dev = nodes // tile
    resident = n_row * nodes * n_col * nodes * 2 <= RESIDENT_BYTES

    source = {m: swap(features, "col", m) for m in far_first(n_col)}
    source[0] = features
    build = densify if resident else densify_far
    dense = build(tile_values, tile_row, tile_col, n_row, n_col, per_dev)

    last = n_col // 2
    last_piece = source.pop(last)
    early = forward_early(dense, source, n_row, resident)

    def late(first, count, dtype):
        return forward_late(dense, early, last, last_piece, first, count, dtype, resident)

    give = late(chips + 1, chips - 1, BF16)
    got = swap(give, "row", 1)
    keep = late(1, chips - 1, F32)
    sends = add_parts(keep, got)
    arrivals = [swap(sends[j - 1], "row", 2 * j) for j in range(1, chips)]
    give_own = late(chips, 1, BF16)
    got_own = swap(give_own, "row", 1)
    keep_own = late(0, 1, F32)
    hidden, neigh_mean, d_pre, d_agg = middle(
        features,
        degree[None, :],
        cotangent,
        w_self,
        w_neigh,
        bias[None, :],
        keep_own,
        got_own,
        arrivals,
    )

    pieces = [d_agg] + [swap(d_agg, "row", 2 * j) for j in range(1, chips)]

    kept, sent = local_grads(features, neigh_mean, d_pre, n_row)
    total = add_sent(kept, swap(sent, "row", 1), BF16)
    mask = n_col // 2
    while mask > 1:
        total = add_sent(total, swap(total, "col", mask), BF16)
        mask //= 2
    pieces, total = lax.optimization_barrier((pieces, total))
    mine = side_by_side(pieces)
    siblings = swap(mine, "row", 1)
    got_last = swap(total, "col", 1)

    early = backward_early(dense, mine, n_col, nodes, resident)
    far_columns, near_columns = list(range(n_col // 2, n_col)), list(range(n_col // 2))
    far = backward_late(dense, early, siblings, far_columns, nodes, resident)
    own, *near = backward_late(dense, early, siblings, near_columns, nodes, resident)
    far_back = tuple(swap(x, "col", m) for m, x in zip(far_columns, far))
    near_back = [swap(x, "col", m) for m, x in zip(near_columns[1:], near)]

    got_last, _ = lax.optimization_barrier((got_last, far))
    cuts = chip_parts(add_sent(total, got_last, F32), n_row)
    arrivals = [swap(cuts[j], "row", 2 * j) for j in range(1, chips)]
    arrivals, _ = lax.optimization_barrier((arrivals, near))
    piece, grad_bias = share_total([cuts[0]] + arrivals)
    shares = join([piece] + [swap(piece, "row", 2 * j) for j in range(1, chips)])
    shares, far_back = lax.optimization_barrier((shares, far_back))
    siblings = swap(shares, "row", 1)
    back = [*near_back, *far_back]
    grad_self, grad_neigh, grad_x = finish(shares, siblings, d_pre, w_self, own, back, n_row)
    return (hidden, grad_x, grad_self, grad_neigh, grad_bias.reshape(width))


def solution(mesh):
    placed = (
        P(("col", "row"), None),
        P(("col", "row")),
        P(("col", "row"), None),
        P(("col", "row"), None, None),
        P(("col", "row")),
        P(("col", "row")),
        P(),
        P(),
        P(),
    )
    return jax.shard_map(
        body,
        mesh=mesh,
        in_specs=placed,
        out_specs=(P(("col", "row"), None), P(("col", "row"), None), P(), P(), P()),
        check_vma=False,
    )
```
